128 devices in a mesh: section: 2 (over y_hi), track: 64 (over x, z, y_lo, core).
Axes of the slice: x: 4, y: 4 (y_hi: 2, y_lo: 2; y = y_hi * 2 + y_lo), z: 4, core: 2. Of those that a mesh axis runs over, the one named last changes fastest.
Arguments:
- raw_echoes: bfloat16 [24576, 512], P(('track', 'section')), may hold values from -6 to 6
- first_target: int32 [64], P('track'), may hold values from 0 to 2047, as said below
- aperture_first: int32 [64], P('track'), may hold values from -2 to 62, as said below
- look_start: int32 [256], P('track'), may hold values from 0 to 2047, as said below
Outputs:
- looks: float32 [256, 256], P('track', 'section')
The draws below stay inside these ranges and needn't reach their ends.
Inputs may be any that keep to these rules, and one draw needn't show every extreme that they name: first_target[j] lies among j * 32 .. j * 32 + 31; the first block's is 0 and the last block's is its largest value. aperture_first[j] is j - 2 or j - 1; the first block's is the former and the last block's the latter. Look l starts inside target block l // 4: look_start[l] lies among (l // 4) * 32 .. (l // 4) * 32 + 31; the first look starts at 0, the last look of the first block at 31, and the last look at 2047.
All inputs are finite; a program needn't handle non-finite values.
Results may differ from the reference program's by a relative error of at most 0.001.
Values may be sent and summed in bfloat16 or wider, within the bound.
No kernel may reach another device: no remote copies, remote signals or barrier semaphores. Data moves between devices by JAX's collectives and lax.ppermute only.
A program may use at most 64 MiB of HBM per device.

```python
import math
import jax
import jax.numpy as jnp
from jax import lax

SAMP = 256
ECH_DEV = 384
TB = 32
LOOK = 16
LPD = 4
HALF_AP = 2
NBLK = 64
NECHO = 24576
NLOOK = 256


def draw_first_target(key, part):
    offsets = jax.random.randint(key, (NBLK,), 0, TB, dtype=jnp.int32)
    offsets = offsets.at[0].set(0).at[NBLK - 1].set(TB - 1)
    return jnp.arange(NBLK, dtype=jnp.int32) * TB + offsets


def draw_aperture_first(key, part):
    offsets = jax.random.randint(key, (NBLK,), 0, 2, dtype=jnp.int32)
    offsets = offsets.at[0].set(0).at[NBLK - 1].set(1)
    return jnp.arange(NBLK, dtype=jnp.int32) - HALF_AP + offsets


def draw_look_start(key, part):
    offsets = jax.random.randint(key, (NLOOK,), 0, TB, dtype=jnp.int32)
    offsets = offsets.at[0].set(0).at[LPD - 1].set(TB - 1).at[NLOOK - 1].set(TB - 1)
    owner_block = jnp.arange(NLOOK, dtype=jnp.int32) // LPD
    return owner_block * TB + offsets


def block_levels(key, shape, shards, least, top_value):
    def one(dim, blocks):
        steps = jax.random.uniform(jax.random.fold_in(jax.random.fold_in(key, 6), dim), (blocks,), jnp.float32, least / len(shards), top_value / len(shards))
        return jnp.repeat(jnp.exp(steps), shape[dim] // blocks).reshape((-1,) + (1,) * (len(shape) - dim - 1))

    level = one(*shards[0])
    for cut in shards[1:]:
        level = level * one(*cut)
    return level


def normal_values(key, extent, scale, bound, cuts=(), kind=jnp.bfloat16):
    result = jax.random.normal(key, extent, jnp.float32) * scale
    if len(cuts) > 0:
        result = block_levels(key, extent, cuts, -0.22, 0.18) * result
    return jnp.clip(result, min=-bound, max=bound).astype(kind)


def setup_inputs(seed: int = 0) -> dict:
    splits = jax.random.split(jax.random.key(seed), 5)
    raw_echoes = normal_values(splits[0], (NECHO, 2 * SAMP), 1.0, 6.0, ((0, 128),))
    first_target = draw_first_target(jax.random.fold_in(splits[4], 71), 0)
    aperture_first = draw_aperture_first(jax.random.fold_in(splits[4], 71), 0)
    look_start = draw_look_start(jax.random.fold_in(splits[4], 71), 0)
    return dict(raw_echoes=raw_echoes, first_target=first_target, aperture_first=aperture_first, look_start=look_start)


BLOCK_LENGTH = 1200.0
ALTITUDE = 1300000.0
WAVE_CENTRE = 568.6
WAVE_SPAN = 13.4
CHIRP_RATE = 0.37
HIGHEST = lax.Precision.HIGHEST

def chirp_phase(samples):
    position = jnp.arange(samples, dtype=jnp.float32) - float(samples // 2)
    return -math.pi * CHIRP_RATE / samples * position * position

def fourier_parts(samples, first_rows, first_cols, count_rows, count_cols):
    row_index = jnp.arange(count_rows, dtype=jnp.int32) + first_rows
    col_index = jnp.arange(count_cols, dtype=jnp.int32) + first_cols
    turns = row_index[:, None] * col_index[None, :] % samples
    angle = turns.astype(jnp.float32) * (2.0 * math.pi / samples)
    factor = 1.0 / math.sqrt(samples)
    return (jnp.cos(angle) * factor, jnp.sin(angle) * factor)

def kernel_sum(signal_real, signal_imag, offset, first_off, wavenumber):
    echo_count = signal_real.shape[0]
    echo_place = BLOCK_LENGTH / ECH_DEV * (offset * echo_count + jnp.arange(echo_count, dtype=jnp.int32)).astype(jnp.float32)
    target_place = BLOCK_LENGTH / TB * (first_off + jnp.arange(TB, dtype=jnp.int32)).astype(jnp.float32)
    along = echo_place[None, :] - target_place[:, None]
    delay = along * along / (jnp.sqrt(ALTITUDE * ALTITUDE + along * along) + ALTITUDE)
    theta = delay[:, :, None] * wavenumber[None, None, :]
    cos_kernel = jnp.cos(theta)
    sin_kernel = jnp.sin(theta)
    real_part = jnp.einsum('tef,ef->tf', cos_kernel, signal_real) + jnp.einsum('tef,ef->tf', sin_kernel, signal_imag)
    imag_part = jnp.einsum('tef,ef->tf', cos_kernel, signal_imag) - jnp.einsum('tef,ef->tf', sin_kernel, signal_real)
    return jnp.concatenate([real_part, imag_part], 1)

def reference(raw_echoes, first_target, aperture_first, look_start):
    raw = raw_echoes.astype(jnp.float32)
    phase = chirp_phase(SAMP)
    rot_cos = jnp.cos(phase)
    rot_sin = jnp.sin(phase)
    raw_real = raw[:, :SAMP]
    raw_imag = raw[:, SAMP:]
    der_real = raw_real * rot_cos - raw_imag * rot_sin
    der_imag = raw_real * rot_sin + raw_imag * rot_cos
    cosine, sine = fourier_parts(SAMP, 0, 0, SAMP, SAMP)
    comp_real = (jnp.dot(der_real, cosine, precision=HIGHEST) + jnp.dot(der_imag, sine, precision=HIGHEST)).astype(jnp.bfloat16)
    comp_imag = (jnp.dot(der_imag, cosine, precision=HIGHEST) - jnp.dot(der_real, sine, precision=HIGHEST)).astype(jnp.bfloat16)
    freq_index = jnp.arange(SAMP, dtype=jnp.int32)
    wavenumber = WAVE_CENTRE + (freq_index.astype(jnp.float32) - float(SAMP // 2)) * (WAVE_SPAN / SAMP)
    offsets = jnp.arange(-HALF_AP, HALF_AP + 1, dtype=jnp.int32)

    def one_block(block_index):
        first_off = first_target[block_index] - block_index * TB
        lowest = aperture_first[block_index]

        def add_block(carried, offset):
            source = block_index + offset
            inside = (source >= 0) & (source < NBLK) & (source >= lowest) & (source < lowest + 2 * HALF_AP)
            start = (jnp.clip(source, 0, NBLK - 1) * ECH_DEV).astype(jnp.int32)
            signal_real = lax.dynamic_slice_in_dim(comp_real, start, ECH_DEV, 0).astype(jnp.float32)
            signal_imag = lax.dynamic_slice_in_dim(comp_imag, start, ECH_DEV, 0).astype(jnp.float32)
            term = kernel_sum(signal_real, signal_imag, offset, first_off, wavenumber)
            return (carried + jnp.where(inside, term, jnp.float32(0.0)), None)
        image, unused = lax.scan(add_block, jnp.zeros((TB, 2 * SAMP), jnp.float32), offsets)
        return image
    images = lax.map(one_block, jnp.arange(NBLK, dtype=jnp.int32))
    images = images.reshape(NBLK * TB, 2 * SAMP) * (1.0 / math.sqrt(2 * HALF_AP * ECH_DEV))
    image_real = images[:, :SAMP]
    image_imag = images[:, SAMP:]
    field_real = jnp.dot(image_real, cosine, precision=HIGHEST) - jnp.dot(image_imag, sine, precision=HIGHEST)
    field_imag = jnp.dot(image_real, sine, precision=HIGHEST) + jnp.dot(image_imag, cosine, precision=HIGHEST)
    power = field_real * field_real + field_imag * field_imag
    padded = jnp.concatenate([power, jnp.zeros((LOOK, SAMP), jnp.float32)], 0)

    def one_look(window_start):
        return lax.optimization_barrier(jnp.sum(lax.dynamic_slice_in_dim(padded, window_start.astype(jnp.int32), LOOK, 0), 0)) / LOOK
    return lax.map(one_look, look_start)
```

```python
import functools
import math

import jax
import jax.numpy as jnp
import numpy as np
from jax import lax
from jax.experimental import pallas as pl
from jax.experimental.pallas import tpu as pltpu
from jax.sharding import PartitionSpec as P

SAMP = 256
ECH_DEV = 384
TB = 32
LOOK = 16
NBLK = 64
STEP = ECH_DEV // TB
HALF = ECH_DEV // 2
SUB = HALF // STEP
ROWS = 192
NFFT = 208
CHUNK = 16
WIN = 80
EXT = 48
VGRP = 4
FWD_AT = 1024
INV_AT = FWD_AT + VGRP * NFFT
RANGE_AT = INV_AT + 4 * ROWS
BF = jnp.bfloat16
F32 = jnp.float32


def split_bf16(x):
    hi = x.astype(np.float32).astype(jnp.bfloat16)
    lo = (x - hi.astype(np.float64)).astype(np.float32).astype(jnp.bfloat16)
    return np.stack([hi, lo])


@functools.lru_cache(maxsize=None)
def tables():
    s = np.arange(SAMP)
    psi = -math.pi * 0.37 * (s - SAMP // 2) ** 2 / SAMP
    turns = np.outer(s, s) % SAMP
    comp = np.exp(1j * psi)[:, None] * np.exp(-2j * math.pi * turns / SAMP) / math.sqrt(SAMP)
    comp = np.block([[comp.real, comp.imag], [-comp.imag, comp.real]])
    comp = split_bf16(comp)

    w = np.arange(NFFT)
    u = np.arange(SUB)
    fwd = np.exp(-2j * math.pi * (np.outer(w, u) % NFFT) / NFFT)
    cols = [[fwd.real, -fwd.imag], [fwd.imag, fwd.real]]
    lhs = np.zeros((VGRP, 2, NFFT, 2, VGRP, SUB))
    for v in range(VGRP):
        for o in range(2):
            for c in range(2):
                lhs[v, o, :, c, v, :] = cols[o][c]
    lhs = lhs.reshape(VGRP * 2 * NFFT, 2 * VGRP * SUB)
    hl = split_bf16(lhs)
    fwd_table = np.concatenate([hl[0], hl[1]], 1)

    f = np.arange(SAMP)
    kappa = 568.6 + (f - SAMP // 2) * 13.4 / SAMP
    resp = []
    for sec in range(2):
        j = sec * SUB - 127 + np.arange(NFFT)
        dist = (STEP * j[None, :] + np.arange(STEP)[:, None]) * (1200.0 / ECH_DEV)
        delay = dist * dist / (np.sqrt(1.3e6 * 1.3e6 + dist * dist) + 1.3e6)
        h = np.exp(-1j * delay[:, :, None] * kappa)
        h = np.roll(h, (sec * SUB - 127) % NFFT, axis=1)
        spec = np.fft.ifft(h, axis=1)
        shift = np.exp(-2j * math.pi * ((w * (SUB * sec + 64)) % NFFT) / NFFT)
        spec = spec * shift[None, :, None] / math.sqrt(4 * ECH_DEV)
        parts = np.stack([spec.real, spec.imag], 1)
        parts = parts.reshape(STEP, 2, NFFT // CHUNK, CHUNK, SAMP)
        resp.append(parts.transpose(2, 0, 1, 3, 4).reshape(NFFT // CHUNK, STEP * 2 * CHUNK, SAMP))
    resp = np.stack(resp).astype(np.float32)

    r = np.arange(ROWS)
    inv = np.exp(2j * math.pi * (np.outer(r, w) % NFFT) / NFFT)
    inv = np.block([[inv.real, -inv.imag], [inv.imag, inv.real]])
    inv_table = split_bf16(inv)

    base = np.exp(2j * math.pi * turns / SAMP) / math.sqrt(SAMP)
    full = np.block([[base.real, base.imag], [-base.imag, base.real]])
    halves = [
        np.concatenate([full[:, h * 128 : h * 128 + 128], full[:, 256 + h * 128 : 384 + h * 128]], 1)
        for h in range(2)
    ]
    range_table = np.stack(
        [split_bf16(np.concatenate([halves[1 - sec], halves[sec]], 1)) for sec in range(2)]
    )
    inv_table = np.concatenate([inv_table, np.zeros((2, 2 * ROWS, 512 - 2 * NFFT), inv_table.dtype)], 2)
    fwd_table = np.concatenate([fwd_table[: VGRP * NFFT], fwd_table[VGRP * NFFT :]], 1)
    packed = [comp, fwd_table, inv_table, range_table]
    return np.concatenate([t.reshape(-1, 512) for t in packed], 0), resp


def dot(a, b):
    return jnp.dot(a, b, preferred_element_type=F32)


def focus_kernel(
    first_ref, low_ref, raw_hbm, tab_hbm, resp_hbm,
    own, mate, up, down,
    raw, comp_t, fwd_t, resp, inv_t, comp, rhs, spec, img, sems,
):
    section = lax.axis_index("section")
    block = lax.axis_index("track")
    chunks = NFFT // CHUNK
    pairs = [(raw_hbm, raw), (tab_hbm.at[:FWD_AT], comp_t), (tab_hbm.at[FWD_AT:INV_AT], fwd_t)]
    pairs += [(resp_hbm.at[section, i], resp.at[i]) for i in range(chunks)]
    pairs += [(tab_hbm.at[INV_AT:RANGE_AT], inv_t)]
    copies = [pltpu.make_async_copy(src, dst, sems.at[i]) for i, (src, dst) in enumerate(pairs)]
    for copy in copies:
        copy.start()
    copies[0].wait()
    copies[1].wait()
    echoes = dot(raw[...], comp_t[:512]) + dot(raw[...], comp_t[512:])
    for n in range(4):
        comp[n] = echoes[:, n * 128 : n * 128 + 128]
    for v in range(STEP):
        rows = [comp[n, pl.ds(v, SUB, stride=STEP), :].astype(BF) for n in range(4)]
        q, i = divmod(v, VGRP)
        for c in range(2):
            part = jnp.concatenate(rows[2 * c : 2 * c + 2], 1)
            for d in range(2):
                at = ((d * 2 + c) * VGRP + i) * SUB
                rhs[q, at : at + SUB, :] = part
    copies[2].wait()
    for q in range(STEP // VGRP):
        for n in range(2):
            spec[q, n * VGRP * NFFT : (n + 1) * VGRP * NFFT] = dot(fwd_t[:, n * SAMP : (n + 1) * SAMP], rhs[q])
    for i in range(chunks):
        copies[3 + i].wait()
        sum_re = jnp.zeros((CHUNK, SAMP), F32)
        sum_im = jnp.zeros((CHUNK, SAMP), F32)
        for v in range(STEP):
            q, k = divmod(v, VGRP)
            at = k * 2 * NFFT + i * CHUNK
            y_re = spec[q, at : at + CHUNK, :]
            y_im = spec[q, at + NFFT : at + NFFT + CHUNK, :]
            h_re = resp[i, v * 2 * CHUNK : v * 2 * CHUNK + CHUNK, :]
            h_im = resp[i, v * 2 * CHUNK + CHUNK : (v + 1) * 2 * CHUNK, :]
            sum_re += y_re * h_re - y_im * h_im
            sum_im += y_re * h_im + y_im * h_re
        for n, total in enumerate((sum_re, sum_im)):
            hi = total.astype(BF)
            at = n * NFFT + i * CHUNK
            img[0, at : at + CHUNK, :] = hi
            img[1, at : at + CHUNK, :] = (total - hi.astype(F32)).astype(BF)
    copies[3 + chunks].wait()
    inv_hi = inv_t[: 2 * ROWS, : 2 * NFFT]
    inv_lo = inv_t[2 * ROWS :, : 2 * NFFT]
    image = dot(inv_hi, img[0]) + (dot(inv_lo, img[0]) + dot(inv_hi, img[1]))
    image = jnp.concatenate([image[:ROWS], image[ROWS:]], 1)
    own[...] = image[64 : 64 + WIN]
    narrow = image.astype(BF)
    up[...] = narrow[96:]
    down[:112, :] = narrow[:112]
    lane = lax.broadcasted_iota(jnp.int32, (16, 2 * SAMP), 1)
    first = (first_ref[0] - block * TB).astype(F32)
    flag = (low_ref[0] - block + 2).astype(F32)
    info = jnp.where(lane < SAMP, first, flag).astype(BF)
    down[112:, :] = info
    mate[:WIN, :] = jnp.where(block % 2 == 0, image[96 : 96 + WIN], image[32 : 32 + WIN]).astype(BF)
    mate[WIN:, :] = info


def join_kernel(low_ref, own, mate, up, down, across, swap_up, swap_down, tab_hbm, send, keep, nxt, table, sem):
    section = lax.axis_index("section")
    block = lax.axis_index("track")
    copy = pltpu.make_async_copy(tab_hbm.at[pl.ds(RANGE_AT + section * 1024, 1024)], table, sem)
    copy.start()
    even = block % 2 == 0
    near_mate = mate[:WIN, :].astype(F32)
    below = jnp.where(even, swap_up[:WIN, :].astype(F32), near_mate)
    above = jnp.where(even, near_mate, swap_down[32:112, :].astype(F32))
    far = jnp.where(even, swap_down[:EXT, :].astype(F32), across[...].astype(F32))
    info = jnp.where(even, mate[WIN:, :].astype(F32), swap_down[112:, :].astype(F32))[:8]
    nxt[...] = info[:, 128:384]
    next_low = info[0:1, SAMP : SAMP + 128] < 0.5
    next_low = jnp.concatenate([next_low] * 4, 1)
    low = low_ref[0] == block - 2
    here = own[...]
    two_up = down[:WIN, :].astype(F32)
    window = below[:64] + here[:64] + above[:64] + jnp.where(low, up[32:, :].astype(F32), two_up[:64])
    beyond = here[32:] + above[32:] + two_up[32:] + jnp.where(next_low, below[32:], far)
    image = jnp.concatenate([window, beyond], 0)
    hi = image.astype(BF)
    lo = (image - hi.astype(F32)).astype(BF)
    copy.wait()
    field = dot(hi, table[:512]) + (dot(lo, table[:512]) + dot(hi, table[512:]))
    send[...] = field[:, :256].astype(BF)
    keep[...] = field[:, 256:]


def look_kernel(first_ref, start_ref, keep, got, nxt, looks):
    block = lax.axis_index("track")
    field = keep[...] + got[...].astype(F32)
    power = field[:, :128] * field[:, :128] + field[:, 128:] * field[:, 128:]
    row = lax.broadcasted_iota(jnp.int32, (64 + EXT, 128), 0)
    next_first = nxt[0:1, 0:128].astype(jnp.int32)
    near = row - (first_ref[0] - block * TB)
    far = row - 64 - next_first + TB
    near = jnp.where((near >= 0) & (near < TB), near, -1)
    far = jnp.where((far >= TB) & (block < NBLK - 1), far, -1)
    place = jnp.where(row < 64, near, far)
    out = []
    for k in range(4):
        start = start_ref[k] - block * TB
        inside = (place >= start) & (place < start + LOOK)
        out.append(jnp.sum(jnp.where(inside, power, 0.0), 0, keepdims=True))
    looks[...] = jnp.concatenate(out, 0) * (1.0 / LOOK)


def shift(value, pairs):
    return lax.ppermute(value, ("section", "track"), pairs)


def both(pairs):
    return [(s * NBLK + a, s * NBLK + b) for s in range(2) for a, b in pairs]


def per_device(tab, resp, raw, first_target, aperture_first, look_start):
    vm = pl.BlockSpec(memory_space=pltpu.VMEM)
    sm = pl.BlockSpec(memory_space=pltpu.SMEM)
    hbm = pl.BlockSpec(memory_space=pltpu.HBM)
    own, mate, up, down = pl.pallas_call(
        focus_kernel,
        out_shape=[
            jax.ShapeDtypeStruct((WIN, 512), F32),
            jax.ShapeDtypeStruct((WIN + 16, 512), BF),
            jax.ShapeDtypeStruct((96, 512), BF),
            jax.ShapeDtypeStruct((128, 512), BF),
        ],
        in_specs=[sm, sm] + [hbm] * 3,
        out_specs=[vm] * 4,
        scratch_shapes=[
            pltpu.VMEM((HALF, 512), BF),
            pltpu.VMEM((FWD_AT, 512), BF),
            pltpu.VMEM((VGRP * NFFT, 512), BF),
            pltpu.VMEM((NFFT // CHUNK, STEP * 2 * CHUNK, SAMP), F32),
            pltpu.VMEM((4 * ROWS, 512), BF),
            pltpu.VMEM((4, HALF, 128), F32),
            pltpu.VMEM((STEP // VGRP, 256, SAMP), BF),
            pltpu.VMEM((STEP // VGRP, VGRP * 2 * NFFT, SAMP), F32),
            pltpu.VMEM((2, 2 * NFFT, SAMP), BF),
            pltpu.SemaphoreType.DMA((NFFT // CHUNK + 4,)),
        ],
        compiler_params=pltpu.CompilerParams(vmem_limit_bytes=52 * 1024 * 1024),
        name="focus",
    )(first_target, aperture_first, raw, tab, resp)
    from_below = shift(up, both([(t, t + 2) for t in range(NBLK - 2)]))
    from_above = shift(down, both([(t, t - 2) for t in range(2, NBLK)]))
    across = shift(down[:EXT], both([(t, t - 3) for t in range(4, NBLK, 2)]))
    swap = both([(t, t ^ 1) for t in range(NBLK)])
    mate = shift(mate, swap)
    swapped = shift(jnp.concatenate([from_below, from_above], 0), swap)
    send, keep, nxt = pl.pallas_call(
        join_kernel,
        out_shape=[
            jax.ShapeDtypeStruct((64 + EXT, 256), BF),
            jax.ShapeDtypeStruct((64 + EXT, 256), F32),
            jax.ShapeDtypeStruct((8, 256), F32),
        ],
        in_specs=[sm] + [vm] * 7 + [hbm],
        out_specs=[vm] * 3,
        scratch_shapes=[pltpu.VMEM((1024, 512), BF), pltpu.SemaphoreType.DMA],
        compiler_params=pltpu.CompilerParams(vmem_limit_bytes=32 * 1024 * 1024),
        name="join",
    )(aperture_first, own, mate, from_below, from_above, across, swapped[:96], swapped[96:], tab)
    got = shift(send, [(s * NBLK + t, (1 - s) * NBLK + t) for s in range(2) for t in range(NBLK)])
    return pl.pallas_call(
        look_kernel,
        out_shape=jax.ShapeDtypeStruct((4, 128), F32),
        in_specs=[sm, sm] + [vm] * 3,
        out_specs=vm,
        compiler_params=pltpu.CompilerParams(vmem_limit_bytes=4 * 1024 * 1024),
        name="look",
    )(first_target, look_start, keep, got, nxt)


def solution(mesh):
    consts = [jnp.asarray(t) for t in tables()]
    body = functools.partial(per_device, *consts)
    return jax.shard_map(
        body,
        mesh=mesh,
        in_specs=(P(("track", "section"), None), P("track"), P("track"), P("track")),
        out_specs=P("track", "section"),
        check_vma=False,
    )
```

```python
import functools
import math

import jax
import jax.numpy as jnp
import numpy as np
from jax import lax
from jax.experimental import pallas as pl
from jax.experimental.pallas import tpu as pltpu
from jax.sharding import PartitionSpec as P

SAMP = 256
ECH_DEV = 384
TB = 32
LOOK = 16
NBLK = 64
STEP = ECH_DEV // TB
HALF = ECH_DEV // 2
SUB = HALF // STEP
ROWS = 192
NFFT = 208
CHUNK = 16
WIN = 80
EXT = 48
VGRP = 4
FWD_AT = 512
INV_AT = FWD_AT + VGRP * NFFT
RANGE_AT = INV_AT + 4 * ROWS
TAB_END = RANGE_AT + 512
FOCUS_VMEM = 54912 * 1024
SMALL_VMEM = 8 * 1024 * 1024
BF = jnp.bfloat16
F32 = jnp.float32


def split_bf16(x):
    hi = x.astype(np.float32).astype(jnp.bfloat16)
    lo = (x - hi.astype(np.float64)).astype(np.float32).astype(jnp.bfloat16)
    return np.stack([hi, lo])


@functools.lru_cache(maxsize=None)
def tables():
    s = np.arange(SAMP)
    psi = -math.pi * 0.37 * (s - SAMP // 2) ** 2 / SAMP
    turns = np.outer(s, s) % SAMP
    comp = np.exp(1j * psi)[:, None] * np.exp(-2j * math.pi * turns / SAMP) / math.sqrt(SAMP)
    comp = split_bf16(np.concatenate([comp.real, comp.imag], 1))

    w = np.arange(NFFT)
    u = np.arange(SUB)
    fwd = np.exp(-2j * math.pi * (np.outer(w, u) % NFFT) / NFFT)
    cols = [[fwd.real, -fwd.imag], [fwd.imag, fwd.real]]
    lhs = np.zeros((VGRP, 2, NFFT, 2, VGRP, SUB))
    for v in range(VGRP):
        for o in range(2):
            for c in range(2):
                lhs[v, o, :, c, v, :] = cols[o][c]
    lhs = lhs.reshape(VGRP * 2 * NFFT, 2 * VGRP * SUB)
    hl = split_bf16(lhs)
    fwd_table = np.concatenate([hl[0], hl[1]], 1)

    f = np.arange(SAMP)
    kappa = 568.6 + (f - SAMP // 2) * 13.4 / SAMP
    resp = []
    for sec in range(2):
        j = sec * SUB - 127 + np.arange(NFFT)
        dist = (STEP * j[None, :] + np.arange(STEP)[:, None]) * (1200.0 / ECH_DEV)
        delay = dist * dist / (np.sqrt(1.3e6 * 1.3e6 + dist * dist) + 1.3e6)
        h = np.exp(-1j * delay[:, :, None] * kappa)
        h = np.roll(h, (sec * SUB - 127) % NFFT, axis=1)
        spec = np.fft.ifft(h, axis=1)
        shift = np.exp(-2j * math.pi * ((w * (SUB * sec + 64)) % NFFT) / NFFT)
        spec = spec * shift[None, :, None] / math.sqrt(4 * ECH_DEV)
        parts = np.stack([spec.real, spec.imag], 1)
        parts = parts.reshape(STEP, 2, NFFT // CHUNK, CHUNK, SAMP)
        resp.append(parts.transpose(2, 0, 1, 3, 4).reshape(NFFT // CHUNK, STEP * 2 * CHUNK, SAMP))
    resp = np.stack(resp).astype(np.float32)

    r = np.arange(ROWS)
    inv = np.exp(2j * math.pi * (np.outer(r, w) % NFFT) / NFFT)
    inv = np.block([[inv.real, -inv.imag], [inv.imag, inv.real]])
    inv_table = split_bf16(inv)

    base = np.exp(2j * math.pi * turns / SAMP) / math.sqrt(SAMP)
    range_table = split_bf16(np.concatenate([base.real, base.imag], 1))
    inv_table = np.concatenate([inv_table, np.zeros((2, 2 * ROWS, 512 - 2 * NFFT), inv_table.dtype)], 2)
    fwd_table = np.concatenate([fwd_table[: VGRP * NFFT], fwd_table[VGRP * NFFT :]], 1)
    packed = [comp, fwd_table, inv_table, range_table]
    return np.concatenate([t.reshape(-1, 512) for t in packed], 0), resp


def dot(a, b):
    return jnp.dot(a, b, preferred_element_type=F32)


def complex_dot(parts, table):
    rows = table.shape[0] // 2
    re, im = parts
    sums = []
    for part in (re, im):
        total = dot(part[0], table[:rows]) + dot(part[0], table[rows:])
        if len(part) > 1:
            total = total + dot(part[1], table[:rows])
        sums.append(total)
    width = table.shape[1] // 2
    return sums[0][:, :width] - sums[1][:, width:], sums[0][:, width:] + sums[1][:, :width]


def hi_lo(x):
    hi = x.astype(BF)
    return hi, (x - hi.astype(F32)).astype(BF)


def focus_kernel(
    raw_hbm, tab_hbm, resp_hbm,
    send, keep,
    raw, comp_t, fwd_t, resp, inv_t, range_t, comp, rhs, spec, img, sems,
):
    section = lax.axis_index("section")
    chunks = NFFT // CHUNK
    pairs = [(raw_hbm, raw), (tab_hbm.at[:FWD_AT], comp_t), (tab_hbm.at[FWD_AT:INV_AT], fwd_t)]
    pairs += [(resp_hbm.at[section, i], resp.at[i]) for i in range(chunks)]
    pairs += [(tab_hbm.at[INV_AT:RANGE_AT], inv_t), (tab_hbm.at[RANGE_AT:TAB_END], range_t)]
    copies = [pltpu.make_async_copy(src, dst, sems.at[i]) for i, (src, dst) in enumerate(pairs)]
    for copy in copies:
        copy.start()
    copies[0].wait()
    copies[1].wait()
    echo_re, echo_im = complex_dot([(raw[:, :SAMP],), (raw[:, SAMP:],)], comp_t[...])
    for n in range(2):
        comp[n] = echo_re[:, n * 128 : n * 128 + 128]
        comp[2 + n] = echo_im[:, n * 128 : n * 128 + 128]
    for v in range(STEP):
        rows = [comp[n, pl.ds(v, SUB, stride=STEP), :].astype(BF) for n in range(4)]
        q, i = divmod(v, VGRP)
        for c in range(2):
            part = jnp.concatenate(rows[2 * c : 2 * c + 2], 1)
            for d in range(2):
                at = ((d * 2 + c) * VGRP + i) * SUB
                rhs[q, at : at + SUB, :] = part
    copies[2].wait()
    for q in range(STEP // VGRP):
        for n in range(2):
            spec[q, n * VGRP * NFFT : (n + 1) * VGRP * NFFT] = dot(fwd_t[:, n * SAMP : (n + 1) * SAMP], rhs[q])
    for i in range(chunks):
        copies[3 + i].wait()
        sum_re = jnp.zeros((CHUNK, SAMP), F32)
        sum_im = jnp.zeros((CHUNK, SAMP), F32)
        for v in range(STEP):
            q, k = divmod(v, VGRP)
            at = k * 2 * NFFT + i * CHUNK
            y_re = spec[q, at : at + CHUNK, :]
            y_im = spec[q, at + NFFT : at + NFFT + CHUNK, :]
            h_re = resp[i, v * 2 * CHUNK : v * 2 * CHUNK + CHUNK, :]
            h_im = resp[i, v * 2 * CHUNK + CHUNK : (v + 1) * 2 * CHUNK, :]
            sum_re += y_re * h_re - y_im * h_im
            sum_im += y_re * h_im + y_im * h_re
        for n, total in enumerate((sum_re, sum_im)):
            hi = total.astype(BF)
            at = n * NFFT + i * CHUNK
            img[0, at : at + CHUNK, :] = hi
            img[1, at : at + CHUNK, :] = (total - hi.astype(F32)).astype(BF)
    copies[3 + chunks].wait()
    inv_hi = inv_t[: 2 * ROWS, : 2 * NFFT]
    inv_lo = inv_t[2 * ROWS :, : 2 * NFFT]
    image = dot(inv_hi, img[0]) + (dot(inv_lo, img[0]) + dot(inv_hi, img[1]))
    copies[4 + chunks].wait()
    field_re, field_im = complex_dot([hi_lo(image[:ROWS]), hi_lo(image[ROWS:])], range_t[...])
    low = jnp.concatenate([field_re[:, :128], field_im[:, :128]], 1)
    high = jnp.concatenate([field_re[:, 128:], field_im[:, 128:]], 1)

    @pl.when(section == 0)
    def low_half():
        send[...] = high.astype(BF)
        keep[...] = low

    @pl.when(section == 1)
    def high_half():
        send[...] = low.astype(BF)
        keep[...] = high


def mix_kernel(first_ref, low_ref, keep, got, own, mine, onward):
    block = lax.axis_index("track")
    lane = lax.broadcasted_iota(jnp.int32, (16, SAMP), 1)
    info = jnp.where(lane < 128, first_ref[0] - block * TB, low_ref[0] - block + 2)
    field = keep[...] + got[...].astype(F32)
    own[...] = field[64 : 64 + WIN]
    mine[112:128, :] = info.astype(F32).astype(BF)

    @pl.when(block % 2 == 0)
    def even():
        onward[...] = field[112:].astype(BF)
        mine[:112, :] = field[:112].astype(BF)
        mine[128:, :] = field[96:176].astype(BF)

    @pl.when(block % 2 == 1)
    def odd():
        onward[...] = field[:80].astype(BF)
        mine[:112, :] = field[80:].astype(BF)
        mine[128:, :] = field[32:112].astype(BF)


def look_kernel(starts, own, mine, mate, moved, swapped, looks):
    block = lax.axis_index("track")
    even = block % 2 == 0
    near = mate[128:, :].astype(F32)
    below = jnp.where(even, moved[96:176, :].astype(F32), near)
    above = jnp.where(even, near, moved[112:192, :].astype(F32))
    two_down = jnp.where(even, moved[16:80, :].astype(F32), swapped[128:192, :].astype(F32))
    two_up = jnp.where(even, swapped[80:160, :].astype(F32), moved[:80, :].astype(F32))
    far = jnp.where(even, swapped[:EXT, :].astype(F32), swapped[192:, :].astype(F32))
    next_info = jnp.where(even, mate[112:128, :].astype(F32), moved[192:, :].astype(F32))
    own_info = mine[112:128, :].astype(F32)
    first, next_first = own_info[0:1, :128], next_info[0:1, :128]
    low, next_low = own_info[0:1, 128:] < 0.5, next_info[0:1, 128:] < 0.5
    low = jnp.concatenate([low, low], 1)
    next_low = jnp.concatenate([next_low, next_low], 1)
    here = own[...]
    window = below[:64] + here[:64] + above[:64] + jnp.where(low, two_down, two_up[:64])
    beyond = here[32:] + above[32:] + two_up[32:] + jnp.where(next_low, below[32:], far)
    field = jnp.concatenate([window, beyond], 0)
    power = field[:, :128] * field[:, :128] + field[:, 128:] * field[:, 128:]
    row = lax.broadcasted_iota(jnp.int32, (64 + EXT, 128), 0)
    inner = row - first.astype(jnp.int32)
    outer = row - 64 - next_first.astype(jnp.int32) + TB
    inner = jnp.where((inner >= 0) & (inner < TB), inner, -1)
    outer = jnp.where((outer >= TB) & (block < NBLK - 1), outer, -1)
    place = jnp.where(row < 64, inner, outer)
    out = []
    for k in range(4):
        start = starts[:, k : k + 1] - block * TB
        inside = (place >= start) & (place < start + LOOK)
        out.append(jnp.sum(jnp.where(inside, power, 0.0), 0, keepdims=True))
    looks[...] = jnp.concatenate(out, 0) * (1.0 / LOOK)


def shift(value, pairs):
    return lax.ppermute(value, ("section", "track"), pairs)


def both(pairs):
    return [(s * NBLK + a, s * NBLK + b) for s in range(2) for a, b in pairs]


def per_device(tab, resp, raw, first_target, aperture_first, look_start):
    vm = pl.BlockSpec(memory_space=pltpu.VMEM)
    sm = pl.BlockSpec(memory_space=pltpu.SMEM)
    hbm = pl.BlockSpec(memory_space=pltpu.HBM)
    send, keep = pl.pallas_call(
        focus_kernel,
        out_shape=[
            jax.ShapeDtypeStruct((ROWS, SAMP), BF),
            jax.ShapeDtypeStruct((ROWS, SAMP), F32),
        ],
        in_specs=[hbm] * 3,
        out_specs=[vm] * 2,
        scratch_shapes=[
            pltpu.VMEM((HALF, 512), BF),
            pltpu.VMEM((FWD_AT, 512), BF),
            pltpu.VMEM((VGRP * NFFT, 512), BF),
            pltpu.VMEM((NFFT // CHUNK, STEP * 2 * CHUNK, SAMP), F32),
            pltpu.VMEM((4 * ROWS, 512), BF),
            pltpu.VMEM((512, 512), BF),
            pltpu.VMEM((4, HALF, 128), F32),
            pltpu.VMEM((STEP // VGRP, 256, SAMP), BF),
            pltpu.VMEM((STEP // VGRP, VGRP * 2 * NFFT, SAMP), F32),
            pltpu.VMEM((2, 2 * NFFT, SAMP), BF),
            pltpu.SemaphoreType.DMA((NFFT // CHUNK + 5,)),
        ],
        compiler_params=pltpu.CompilerParams(vmem_limit_bytes=FOCUS_VMEM),
        name="focus",
    )(raw, tab, resp)
    first_target, aperture_first, look_start, keep = lax.optimization_barrier(
        (first_target, aperture_first, look_start, keep)
    )
    got = shift(send, [(s * NBLK + t, (1 - s) * NBLK + t) for s in range(2) for t in range(NBLK)])
    own, mine, onward = pl.pallas_call(
        mix_kernel,
        out_shape=[
            jax.ShapeDtypeStruct((WIN, SAMP), F32),
            jax.ShapeDtypeStruct((208, SAMP), BF),
            jax.ShapeDtypeStruct((80, SAMP), BF),
        ],
        in_specs=[sm] * 2 + [vm] * 2,
        out_specs=[vm] * 3,
        compiler_params=pltpu.CompilerParams(vmem_limit_bytes=SMALL_VMEM),
        name="mix",
    )(first_target, aperture_first, keep, got)
    swap = both([(t, t ^ 1) for t in range(NBLK)])
    mate = shift(mine, swap)
    moved = shift(
        jnp.concatenate([onward, mate[:128]], 0),
        both([(t, t + 2) for t in range(0, NBLK - 2, 2)] + [(t, t - 2) for t in range(3, NBLK, 2)]),
    )
    across = shift(mine[:EXT], both([(t, t - 4) for t in range(4, NBLK, 2)]))
    swapped = shift(jnp.concatenate([moved[:192], across], 0), swap)
    return pl.pallas_call(
        look_kernel,
        out_shape=jax.ShapeDtypeStruct((4, 128), F32),
        in_specs=[vm] * 6,
        out_specs=vm,
        compiler_params=pltpu.CompilerParams(vmem_limit_bytes=SMALL_VMEM),
        name="look",
    )(look_start.reshape(1, 4), own, mine, mate, moved, swapped)


def solution(mesh):
    consts = [jnp.asarray(t) for t in tables()]
    body = functools.partial(per_device, *consts)
    return jax.shard_map(
        body,
        mesh=mesh,
        in_specs=(P(("track", "section"), None), P("track"), P("track"), P("track")),
        out_specs=P("track", "section"),
        check_vma=False,
    )
```

```python
import functools
import math

import jax
import jax.numpy as jnp
import numpy as np
from jax import lax
from jax.experimental import pallas as pl
from jax.experimental.pallas import tpu as pltpu
from jax.sharding import PartitionSpec as P

SAMP = 256
ECH_DEV = 384
TB = 32
LOOK = 16
NBLK = 64
STEP = ECH_DEV // TB
HALF = ECH_DEV // 2
SUB = HALF // STEP
ROWS = 192
WINDOWS = 2
WROWS = ROWS // WINDOWS
NFFT = WROWS + SUB
CHUNK = 16
CHUNKS = WINDOWS * NFFT // CHUNK
WIN = 80
EXT = 48
VGRP = 4
FWD_AT = 512
INV_AT = FWD_AT + VGRP * NFFT
RANGE_AT = INV_AT + 2 * WROWS
TAB_END = RANGE_AT + 512
FOCUS_VMEM = 54912 * 1024
SMALL_VMEM = 8 * 1024 * 1024
BF = jnp.bfloat16
F32 = jnp.float32


def split_bf16(x):
    hi = x.astype(np.float32).astype(jnp.bfloat16)
    lo = (x - hi.astype(np.float64)).astype(np.float32).astype(jnp.bfloat16)
    return np.stack([hi, lo])


@functools.lru_cache(maxsize=None)
def tables():
    s = np.arange(SAMP)
    psi = -math.pi * 0.37 * (s - SAMP // 2) ** 2 / SAMP
    turns = np.outer(s, s) % SAMP
    comp = np.exp(1j * psi)[:, None] * np.exp(-2j * math.pi * turns / SAMP) / math.sqrt(SAMP)
    comp = split_bf16(np.concatenate([comp.real, comp.imag], 1))

    w = np.arange(NFFT)
    u = np.arange(SUB)
    fwd = np.exp(-2j * math.pi * (np.outer(w, u) % NFFT) / NFFT)
    cols = [[fwd.real, -fwd.imag], [fwd.imag, fwd.real]]
    lhs = np.zeros((VGRP, 2, NFFT, 2, VGRP, SUB))
    for v in range(VGRP):
        for o in range(2):
            for c in range(2):
                lhs[v, o, :, c, v, :] = cols[o][c]
    lhs = lhs.reshape(VGRP * 2 * NFFT, 2 * VGRP * SUB)
    hl = split_bf16(lhs)
    fwd_table = np.concatenate([hl[0], hl[1]], 1)

    f = np.arange(SAMP)
    kappa = 568.6 + (f - SAMP // 2) * 13.4 / SAMP
    resp = []
    for sec in range(2):
        for win in range(WINDOWS):
            m = np.arange(-WROWS, SUB)
            j = sec * SUB + 64 - win * WROWS + m
            dist = (STEP * j[None, :] + np.arange(STEP)[:, None]) * (1200.0 / ECH_DEV)
            delay = dist * dist / (np.sqrt(1.3e6 * 1.3e6 + dist * dist) + 1.3e6)
            h = np.exp(-1j * delay[:, :, None] * kappa)
            h = np.roll(h, -WROWS, axis=1)
            spec = np.fft.ifft(h, axis=1) / math.sqrt(4 * ECH_DEV)
            parts = np.stack([spec.real, spec.imag], 1)
            parts = parts.reshape(STEP, 2, NFFT // CHUNK, CHUNK, SAMP)
            resp.append(parts.transpose(2, 0, 1, 3, 4).reshape(NFFT // CHUNK, STEP * 2 * CHUNK, SAMP))
    resp = np.stack(resp).astype(np.float32).reshape(2, CHUNKS, STEP * 2 * CHUNK, SAMP)

    r = np.arange(WROWS)
    inv = np.exp(2j * math.pi * (np.outer(r, w) % NFFT) / NFFT)
    inv = np.block([[inv.real, -inv.imag], [inv.imag, inv.real]])
    inv_table = np.zeros((2 * WROWS, 2, SAMP), jnp.bfloat16)
    inv_table[:, :, : 2 * NFFT] = split_bf16(inv).transpose(1, 0, 2)

    base = np.exp(2j * math.pi * turns / SAMP) / math.sqrt(SAMP)
    range_table = split_bf16(np.concatenate([base.real, base.imag], 1))
    fwd_table = np.concatenate([fwd_table[: VGRP * NFFT], fwd_table[VGRP * NFFT :]], 1)
    packed = [comp, fwd_table, inv_table, range_table]
    return np.concatenate([t.reshape(-1, 512) for t in packed], 0), resp


def dot(a, b):
    return jnp.dot(a, b, preferred_element_type=F32)


def complex_dot(parts, table):
    rows = table.shape[0] // 2
    re, im = parts
    sums = []
    for part in (re, im):
        total = dot(part[0], table[:rows]) + dot(part[0], table[rows:])
        if len(part) > 1:
            total = total + dot(part[1], table[:rows])
        sums.append(total)
    width = table.shape[1] // 2
    return sums[0][:, :width] - sums[1][:, width:], sums[0][:, width:] + sums[1][:, :width]


def hi_lo(x):
    hi = x.astype(BF)
    return hi, (x - hi.astype(F32)).astype(BF)


def focus_kernel(
    raw_hbm, tab_hbm, resp_hbm,
    send, keep,
    raw, comp_t, fwd_t, resp, inv_t, range_t, comp, rhs, spec, img, sems,
):
    section = lax.axis_index("section")
    chunks = CHUNKS
    pairs = [(raw_hbm, raw), (tab_hbm.at[:FWD_AT], comp_t), (tab_hbm.at[FWD_AT:INV_AT], fwd_t)]
    pairs += [(resp_hbm.at[section, i], resp.at[i]) for i in range(chunks)]
    pairs += [(tab_hbm.at[INV_AT:RANGE_AT], inv_t), (tab_hbm.at[RANGE_AT:TAB_END], range_t)]
    pairs = pairs[:3] + pairs[-2:] + pairs[3:-2]
    copies = [pltpu.make_async_copy(src, dst, sems.at[i]) for i, (src, dst) in enumerate(pairs)]
    for copy in copies:
        copy.start()
    copies[0].wait()
    copies[1].wait()
    echo_re, echo_im = complex_dot([(raw[:, :SAMP],), (raw[:, SAMP:],)], comp_t[...])
    for n in range(2):
        comp[n] = echo_re[:, n * 128 : n * 128 + 128]
        comp[2 + n] = echo_im[:, n * 128 : n * 128 + 128]
    for v in range(STEP):
        rows = [comp[n, pl.ds(v, SUB, stride=STEP), :].astype(BF) for n in range(4)]
        q, i = divmod(v, VGRP)
        for c in range(2):
            part = jnp.concatenate(rows[2 * c : 2 * c + 2], 1)
            for d in range(2):
                at = ((d * 2 + c) * VGRP + i) * SUB
                rhs[q, at : at + SUB, :] = part
    copies[2].wait()
    for q in range(STEP // VGRP):
        for n in range(2):
            spec[q, n * VGRP * NFFT : (n + 1) * VGRP * NFFT] = dot(fwd_t[:, n * SAMP : (n + 1) * SAMP], rhs[q])
    copies[3].wait()
    copies[4].wait()
    inv_hi = inv_t[:, : 2 * NFFT]
    inv_lo = inv_t[:, SAMP : SAMP + 2 * NFFT]
    image = []
    for i in range(chunks):
        win, j = divmod(i, NFFT // CHUNK)
        copies[5 + i].wait()
        sum_re = jnp.zeros((CHUNK, SAMP), F32)
        sum_im = jnp.zeros((CHUNK, SAMP), F32)
        for v in range(STEP):
            q, k = divmod(v, VGRP)
            at = k * 2 * NFFT + j * CHUNK
            y_re = spec[q, at : at + CHUNK, :]
            y_im = spec[q, at + NFFT : at + NFFT + CHUNK, :]
            h_re = resp[i, v * 2 * CHUNK : v * 2 * CHUNK + CHUNK, :]
            h_im = resp[i, v * 2 * CHUNK + CHUNK : (v + 1) * 2 * CHUNK, :]
            sum_re += y_re * h_re - y_im * h_im
            sum_im += y_re * h_im + y_im * h_re
        for n, total in enumerate((sum_re, sum_im)):
            at = n * NFFT + j * CHUNK
            img[win, 0, at : at + CHUNK, :], img[win, 1, at : at + CHUNK, :] = hi_lo(total)
        if j == NFFT // CHUNK - 1:
            image.append(dot(inv_hi, img[win, 0]) + (dot(inv_lo, img[win, 0]) + dot(inv_hi, img[win, 1])))
    image_re = jnp.concatenate([part[:WROWS] for part in image], 0)
    image_im = jnp.concatenate([part[WROWS:] for part in image], 0)
    field_re, field_im = complex_dot([hi_lo(image_re), hi_lo(image_im)], range_t[...])
    low = jnp.concatenate([field_re[:, :128], field_im[:, :128]], 1)
    high = jnp.concatenate([field_re[:, 128:], field_im[:, 128:]], 1)

    @pl.when(section == 0)
    def low_half():
        send[...] = high.astype(BF)
        keep[...] = low

    @pl.when(section == 1)
    def high_half():
        send[...] = low.astype(BF)
        keep[...] = high


def mix_kernel(first_ref, low_ref, keep, got, own, mine, onward):
    block = lax.axis_index("track")
    lane = lax.broadcasted_iota(jnp.int32, (16, SAMP), 1)
    info = jnp.where(lane < 128, first_ref[0] - block * TB, low_ref[0] - block + 2)
    field = keep[...] + got[...].astype(F32)
    own[...] = field[64 : 64 + WIN]
    mine[112:128, :] = info.astype(F32).astype(BF)

    @pl.when(block % 2 == 0)
    def even():
        onward[...] = field[112:].astype(BF)
        mine[:112, :] = field[:112].astype(BF)
        mine[128:, :] = field[96:176].astype(BF)

    @pl.when(block % 2 == 1)
    def odd():
        onward[...] = field[:80].astype(BF)
        mine[:112, :] = field[80:].astype(BF)
        mine[128:, :] = field[32:112].astype(BF)


def look_kernel(starts, own, mine, mate, moved, swapped, looks):
    block = lax.axis_index("track")
    even = block % 2 == 0
    near = mate[128:, :].astype(F32)
    below = jnp.where(even, moved[96:176, :].astype(F32), near)
    above = jnp.where(even, near, moved[112:192, :].astype(F32))
    two_down = jnp.where(even, moved[16:80, :].astype(F32), swapped[128:192, :].astype(F32))
    two_up = jnp.where(even, swapped[80:160, :].astype(F32), moved[:80, :].astype(F32))
    far = jnp.where(even, swapped[:EXT, :].astype(F32), swapped[192:, :].astype(F32))
    next_info = jnp.where(even, mate[112:128, :].astype(F32), moved[192:, :].astype(F32))
    own_info = mine[112:128, :].astype(F32)
    first, next_first = own_info[0:1, :128], next_info[0:1, :128]
    low, next_low = own_info[0:1, 128:] < 0.5, next_info[0:1, 128:] < 0.5
    low = jnp.concatenate([low, low], 1)
    next_low = jnp.concatenate([next_low, next_low], 1)
    here = own[...]
    window = below[:64] + here[:64] + above[:64] + jnp.where(low, two_down, two_up[:64])
    beyond = here[32:] + above[32:] + two_up[32:] + jnp.where(next_low, below[32:], far)
    field = jnp.concatenate([window, beyond], 0)
    power = field[:, :128] * field[:, :128] + field[:, 128:] * field[:, 128:]
    row = lax.broadcasted_iota(jnp.int32, (64 + EXT, 128), 0)
    inner = row - first.astype(jnp.int32)
    outer = row - 64 - next_first.astype(jnp.int32) + TB
    inner = jnp.where((inner >= 0) & (inner < TB), inner, -1)
    outer = jnp.where((outer >= TB) & (block < NBLK - 1), outer, -1)
    place = jnp.where(row < 64, inner, outer)
    out = []
    for k in range(4):
        start = starts[:, k : k + 1] - block * TB
        inside = (place >= start) & (place < start + LOOK)
        out.append(jnp.sum(jnp.where(inside, power, 0.0), 0, keepdims=True))
    looks[...] = jnp.concatenate(out, 0) * (1.0 / LOOK)


def shift(value, pairs):
    return lax.ppermute(value, ("section", "track"), pairs)


def both(pairs):
    return [(s * NBLK + a, s * NBLK + b) for s in range(2) for a, b in pairs]


def per_device(tab, resp, raw, first_target, aperture_first, look_start):
    vm = pl.BlockSpec(memory_space=pltpu.VMEM)
    sm = pl.BlockSpec(memory_space=pltpu.SMEM)
    hbm = pl.BlockSpec(memory_space=pltpu.HBM)
    send, keep = pl.pallas_call(
        focus_kernel,
        out_shape=[
            jax.ShapeDtypeStruct((ROWS, SAMP), BF),
            jax.ShapeDtypeStruct((ROWS, SAMP), F32),
        ],
        in_specs=[hbm] * 3,
        out_specs=[vm] * 2,
        scratch_shapes=[
            pltpu.VMEM((HALF, 512), BF),
            pltpu.VMEM((FWD_AT, 512), BF),
            pltpu.VMEM((VGRP * NFFT, 512), BF),
            pltpu.VMEM((CHUNKS, STEP * 2 * CHUNK, SAMP), F32),
            pltpu.VMEM((2 * WROWS, 512), BF),
            pltpu.VMEM((512, 512), BF),
            pltpu.VMEM((4, HALF, 128), F32),
            pltpu.VMEM((STEP // VGRP, 256, SAMP), BF),
            pltpu.VMEM((STEP // VGRP, VGRP * 2 * NFFT, SAMP), F32),
            pltpu.VMEM((WINDOWS, 2, 2 * NFFT, SAMP), BF),
            pltpu.SemaphoreType.DMA((CHUNKS + 5,)),
        ],
        compiler_params=pltpu.CompilerParams(vmem_limit_bytes=FOCUS_VMEM),
        name="focus",
    )(raw, tab, resp)
    first_target, aperture_first, look_start, keep = lax.optimization_barrier(
        (first_target, aperture_first, look_start, keep)
    )
    got = shift(send, [(s * NBLK + t, (1 - s) * NBLK + t) for s in range(2) for t in range(NBLK)])
    own, mine, onward = pl.pallas_call(
        mix_kernel,
        out_shape=[
            jax.ShapeDtypeStruct((WIN, SAMP), F32),
            jax.ShapeDtypeStruct((208, SAMP), BF),
            jax.ShapeDtypeStruct((80, SAMP), BF),
        ],
        in_specs=[sm] * 2 + [vm] * 2,
        out_specs=[vm] * 3,
        compiler_params=pltpu.CompilerParams(vmem_limit_bytes=SMALL_VMEM),
        name="mix",
    )(first_target, aperture_first, keep, got)
    swap = both([(t, t ^ 1) for t in range(NBLK)])
    mate = shift(mine, swap)
    moved = shift(
        jnp.concatenate([onward, mate[:128]], 0),
        both([(t, t + 2) for t in range(0, NBLK - 2, 2)] + [(t, t - 2) for t in range(3, NBLK, 2)]),
    )
    across = shift(mine[:EXT], both([(t, t - 4) for t in range(4, NBLK, 2)]))
    swapped = shift(jnp.concatenate([moved[:192], across], 0), swap)
    return pl.pallas_call(
        look_kernel,
        out_shape=jax.ShapeDtypeStruct((4, 128), F32),
        in_specs=[vm] * 6,
        out_specs=vm,
        compiler_params=pltpu.CompilerParams(vmem_limit_bytes=SMALL_VMEM),
        name="look",
    )(look_start.reshape(1, 4), own, mine, mate, moved, swapped)


def solution(mesh):
    consts = [jnp.asarray(t) for t in tables()]
    body = functools.partial(per_device, *consts)
    return jax.shard_map(
        body,
        mesh=mesh,
        in_specs=(P(("track", "section"), None), P("track"), P("track"), P("track")),
        out_specs=P("track", "section"),
        check_vma=False,
    )
```

```python
import functools
import math

import jax
import jax.numpy as jnp
import numpy as np
from jax import lax
from jax.experimental import pallas as pl
from jax.experimental.pallas import tpu as pltpu
from jax.sharding import PartitionSpec as P

SAMP = 256
ECH_DEV = 384
TB = 32
LOOK = 16
NBLK = 64
STEP = ECH_DEV // TB
HALF = ECH_DEV // 2
SUB = HALF // STEP
ROWS = 192
WINDOWS = 2
WROWS = ROWS // WINDOWS
NFFT = WROWS + SUB
CHUNK = 16
CHUNKS = WINDOWS * NFFT // CHUNK
WIN = 80
EXT = 48
VGRP = 4
TOP_CHIPS = 8
FWD_AT = 512
INV_AT = FWD_AT + VGRP * NFFT
RANGE_AT = INV_AT + 2 * WROWS
TAB_END = RANGE_AT + 512
FOCUS_VMEM = 54912 * 1024
SMALL_VMEM = 8 * 1024 * 1024
BF = jnp.bfloat16
F32 = jnp.float32


def split_bf16(x):
    hi = x.astype(np.float32).astype(jnp.bfloat16)
    lo = (x - hi.astype(np.float64)).astype(np.float32).astype(jnp.bfloat16)
    return np.stack([hi, lo])


@functools.lru_cache(maxsize=None)
def tables():
    s = np.arange(SAMP)
    psi = -math.pi * 0.37 * (s - SAMP // 2) ** 2 / SAMP
    turns = np.outer(s, s) % SAMP
    comp = np.exp(1j * psi)[:, None] * np.exp(-2j * math.pi * turns / SAMP) / math.sqrt(SAMP)
    comp = split_bf16(np.concatenate([comp.real, comp.imag], 1))

    w = np.arange(NFFT)
    u = np.arange(SUB)
    fwd = np.exp(-2j * math.pi * (np.outer(w, u) % NFFT) / NFFT)
    cols = [[fwd.real, -fwd.imag], [fwd.imag, fwd.real]]
    lhs = np.zeros((VGRP, 2, NFFT, 2, VGRP, SUB))
    for v in range(VGRP):
        for o in range(2):
            for c in range(2):
                lhs[v, o, :, c, v, :] = cols[o][c]
    lhs = lhs.reshape(VGRP * 2 * NFFT, 2 * VGRP * SUB)
    hl = split_bf16(lhs)
    fwd_table = np.concatenate([hl[0], hl[1]], 1)

    f = np.arange(SAMP)
    kappa = 568.6 + (f - SAMP // 2) * 13.4 / SAMP
    resp = []
    for sec in range(2):
        for win in range(WINDOWS):
            m = np.arange(-WROWS, SUB)
            j = sec * SUB + 64 - win * WROWS + m
            dist = (STEP * j[None, :] + np.arange(STEP)[:, None]) * (1200.0 / ECH_DEV)
            delay = dist * dist / (np.sqrt(1.3e6 * 1.3e6 + dist * dist) + 1.3e6)
            h = np.exp(-1j * delay[:, :, None] * kappa)
            h = np.roll(h, -WROWS, axis=1)
            spec = np.fft.ifft(h, axis=1) / math.sqrt(4 * ECH_DEV)
            parts = np.stack([spec.real, spec.imag], 1)
            parts = parts.reshape(STEP, 2, NFFT // CHUNK, CHUNK, SAMP)
            resp.append(parts.transpose(2, 0, 1, 3, 4).reshape(NFFT // CHUNK, STEP * 2 * CHUNK, SAMP))
    resp = np.stack(resp).astype(np.float32).reshape(2, CHUNKS, STEP * 2 * CHUNK, SAMP)

    r = np.arange(WROWS)
    inv = np.exp(2j * math.pi * (np.outer(r, w) % NFFT) / NFFT)
    inv = np.block([[inv.real, -inv.imag], [inv.imag, inv.real]])
    inv_table = np.zeros((2 * WROWS, 2, SAMP), jnp.bfloat16)
    inv_table[:, :, : 2 * NFFT] = split_bf16(inv).transpose(1, 0, 2)

    base = np.exp(2j * math.pi * turns / SAMP) / math.sqrt(SAMP)
    range_table = split_bf16(np.concatenate([base.real, base.imag], 1))
    fwd_table = np.concatenate([fwd_table[: VGRP * NFFT], fwd_table[VGRP * NFFT :]], 1)
    packed = [comp, fwd_table, inv_table, range_table]
    return np.concatenate([t.reshape(-1, 512) for t in packed], 0), resp


def dot(a, b):
    return jnp.dot(a, b, preferred_element_type=F32)


def complex_dot(parts, table):
    rows = table.shape[0] // 2
    re, im = parts
    sums = []
    for part in (re, im):
        total = dot(part[0], table[:rows]) + dot(part[0], table[rows:])
        if len(part) > 1:
            total = total + dot(part[1], table[:rows])
        sums.append(total)
    width = table.shape[1] // 2
    return sums[0][:, :width] - sums[1][:, width:], sums[0][:, width:] + sums[1][:, :width]


def hi_lo(x):
    hi = x.astype(BF)
    return hi, (x - hi.astype(F32)).astype(BF)


def focus_kernel(
    raw_hbm, tab_hbm, resp_hbm,
    send, keep,
    raw, comp_t, fwd_t, resp, inv_t, range_t, comp, rhs, spec, img, sems,
):
    section = lax.axis_index("section")
    chunks = CHUNKS
    pairs = [(raw_hbm, raw), (tab_hbm.at[:FWD_AT], comp_t), (tab_hbm.at[FWD_AT:INV_AT], fwd_t)]
    pairs += [(resp_hbm.at[section, i], resp.at[i]) for i in range(chunks)]
    pairs += [(tab_hbm.at[INV_AT:RANGE_AT], inv_t), (tab_hbm.at[RANGE_AT:TAB_END], range_t)]
    pairs = pairs[:3] + pairs[-2:] + pairs[3:-2]
    copies = [pltpu.make_async_copy(src, dst, sems.at[i]) for i, (src, dst) in enumerate(pairs)]
    for copy in copies:
        copy.start()
    copies[0].wait()
    copies[1].wait()
    echo_re, echo_im = complex_dot([(raw[:, :SAMP],), (raw[:, SAMP:],)], comp_t[...])
    for n in range(2):
        comp[n] = echo_re[:, n * 128 : n * 128 + 128]
        comp[2 + n] = echo_im[:, n * 128 : n * 128 + 128]
    for v in range(STEP):
        rows = [comp[n, pl.ds(v, SUB, stride=STEP), :].astype(BF) for n in range(4)]
        q, i = divmod(v, VGRP)
        for c in range(2):
            part = jnp.concatenate(rows[2 * c : 2 * c + 2], 1)
            for d in range(2):
                at = ((d * 2 + c) * VGRP + i) * SUB
                rhs[q, at : at + SUB, :] = part
    copies[2].wait()
    for q in range(STEP // VGRP):
        for n in range(2):
            spec[q, n * VGRP * NFFT : (n + 1) * VGRP * NFFT] = dot(fwd_t[:, n * SAMP : (n + 1) * SAMP], rhs[q])
    copies[3].wait()
    copies[4].wait()
    inv_hi = inv_t[:, : 2 * NFFT]
    inv_lo = inv_t[:, SAMP : SAMP + 2 * NFFT]
    image = []
    for i in range(chunks):
        win, j = divmod(i, NFFT // CHUNK)
        copies[5 + i].wait()
        sum_re = jnp.zeros((CHUNK, SAMP), F32)
        sum_im = jnp.zeros((CHUNK, SAMP), F32)
        for v in range(STEP):
            q, k = divmod(v, VGRP)
            at = k * 2 * NFFT + j * CHUNK
            y_re = spec[q, at : at + CHUNK, :]
            y_im = spec[q, at + NFFT : at + NFFT + CHUNK, :]
            h_re = resp[i, v * 2 * CHUNK : v * 2 * CHUNK + CHUNK, :]
            h_im = resp[i, v * 2 * CHUNK + CHUNK : (v + 1) * 2 * CHUNK, :]
            sum_re += y_re * h_re - y_im * h_im
            sum_im += y_re * h_im + y_im * h_re
        for n, total in enumerate((sum_re, sum_im)):
            at = n * NFFT + j * CHUNK
            img[win, 0, at : at + CHUNK, :], img[win, 1, at : at + CHUNK, :] = hi_lo(total)
        if j == NFFT // CHUNK - 1:
            image.append(dot(inv_hi, img[win, 0]) + (dot(inv_lo, img[win, 0]) + dot(inv_hi, img[win, 1])))
    image_re = jnp.concatenate([part[:WROWS] for part in image], 0)
    image_im = jnp.concatenate([part[WROWS:] for part in image], 0)
    field_re, field_im = complex_dot([hi_lo(image_re), hi_lo(image_im)], range_t[...])
    low = jnp.concatenate([field_re[:, :128], field_im[:, :128]], 1)
    high = jnp.concatenate([field_re[:, 128:], field_im[:, 128:]], 1)

    @pl.when(section == 0)
    def low_half():
        send[...] = high.astype(BF)
        keep[...] = low

    @pl.when(section == 1)
    def high_half():
        send[...] = low.astype(BF)
        keep[...] = high


def mix_kernel(first_ref, low_ref, keep, got, own, mine, onward):
    block = lax.axis_index("track")
    lane = lax.broadcasted_iota(jnp.int32, (16, SAMP), 1)
    info = jnp.where(lane < 128, first_ref[0] - block * TB, low_ref[0] - block + 2)
    field = keep[...] + got[...].astype(F32)
    own[...] = field[64 : 64 + WIN]
    mine[112:128, :] = info.astype(F32).astype(BF)

    @pl.when(block % 2 == 0)
    def even():
        onward[...] = field[112:].astype(BF)
        mine[:112, :] = field[:112].astype(BF)
        mine[128:, :] = field[96:176].astype(BF)

    @pl.when(block % 2 == 1)
    def odd():
        onward[...] = field[:80].astype(BF)
        mine[:112, :] = field[80:].astype(BF)
        mine[128:, :] = field[32:112].astype(BF)


def look_kernel(starts, own, mine, mate, moved, swapped, looks):
    block = lax.axis_index("track")
    even = block % 2 == 0
    near = mate[128:, :].astype(F32)
    below = jnp.where(even, moved[96:176, :].astype(F32), near)
    above = jnp.where(even, near, moved[112:192, :].astype(F32))
    two_down = jnp.where(even, moved[16:80, :].astype(F32), swapped[128:192, :].astype(F32))
    two_up = jnp.where(even, swapped[80:160, :].astype(F32), moved[:80, :].astype(F32))
    far = jnp.where(even, swapped[:EXT, :].astype(F32), swapped[192:, :].astype(F32))
    next_info = jnp.where(even, mate[112:128, :].astype(F32), moved[192:, :].astype(F32))
    own_info = mine[112:128, :].astype(F32)
    first, next_first = own_info[0:1, :128], next_info[0:1, :128]
    low, next_low = own_info[0:1, 128:] < 0.5, next_info[0:1, 128:] < 0.5
    low = jnp.concatenate([low, low], 1)
    next_low = jnp.concatenate([next_low, next_low], 1)
    here = own[...]
    window = below[:64] + here[:64] + above[:64] + jnp.where(low, two_down, two_up[:64])
    beyond = here[32:] + above[32:] + two_up[32:] + jnp.where(next_low, below[32:], far)
    field = jnp.concatenate([window, beyond], 0)
    power = field[:, :128] * field[:, :128] + field[:, 128:] * field[:, 128:]
    row = lax.broadcasted_iota(jnp.int32, (64 + EXT, 128), 0)
    inner = row - first.astype(jnp.int32)
    outer = row - 64 - next_first.astype(jnp.int32) + TB
    inner = jnp.where((inner >= 0) & (inner < TB), inner, -1)
    outer = jnp.where((outer >= TB) & (block < NBLK - 1), outer, -1)
    place = jnp.where(row < 64, inner, outer)
    out = []
    for k in range(4):
        start = starts[:, k : k + 1] - block * TB
        inside = (place >= start) & (place < start + LOOK)
        out.append(jnp.sum(jnp.where(inside, power, 0.0), 0, keepdims=True))
    looks[...] = jnp.concatenate(out, 0) * (1.0 / LOOK)


def shift(value, pairs):
    return lax.ppermute(value, ("section", "track"), pairs)


def both(pairs):
    return [(s * NBLK + a, s * NBLK + b) for s in range(2) for a, b in pairs]


def per_device(tab, resp, raw, first_target, aperture_first, look_start):
    vm = pl.BlockSpec(memory_space=pltpu.VMEM)
    sm = pl.BlockSpec(memory_space=pltpu.SMEM)
    hbm = pl.BlockSpec(memory_space=pltpu.HBM)
    send, keep = pl.pallas_call(
        focus_kernel,
        out_shape=[
            jax.ShapeDtypeStruct((ROWS, SAMP), BF),
            jax.ShapeDtypeStruct((ROWS, SAMP), F32),
        ],
        in_specs=[hbm] * 3,
        out_specs=[vm] * 2,
        scratch_shapes=[
            pltpu.VMEM((HALF, 512), BF),
            pltpu.VMEM((FWD_AT, 512), BF),
            pltpu.VMEM((VGRP * NFFT, 512), BF),
            pltpu.VMEM((CHUNKS, STEP * 2 * CHUNK, SAMP), F32),
            pltpu.VMEM((2 * WROWS, 512), BF),
            pltpu.VMEM((512, 512), BF),
            pltpu.VMEM((4, HALF, 128), F32),
            pltpu.VMEM((STEP // VGRP, 256, SAMP), BF),
            pltpu.VMEM((STEP // VGRP, VGRP * 2 * NFFT, SAMP), F32),
            pltpu.VMEM((WINDOWS, 2, 2 * NFFT, SAMP), BF),
            pltpu.SemaphoreType.DMA((CHUNKS + 5,)),
        ],
        compiler_params=pltpu.CompilerParams(vmem_limit_bytes=FOCUS_VMEM),
        name="focus",
    )(raw, tab, resp)
    first_target, aperture_first, look_start, keep = lax.optimization_barrier(
        (first_target, aperture_first, look_start, keep)
    )
    got = shift(send, [(s * NBLK + t, (1 - s) * NBLK + t) for s in range(2) for t in range(NBLK)])
    own, mine, onward = pl.pallas_call(
        mix_kernel,
        out_shape=[
            jax.ShapeDtypeStruct((WIN, SAMP), F32),
            jax.ShapeDtypeStruct((208, SAMP), BF),
            jax.ShapeDtypeStruct((80, SAMP), BF),
        ],
        in_specs=[sm] * 2 + [vm] * 2,
        out_specs=[vm] * 3,
        compiler_params=pltpu.CompilerParams(vmem_limit_bytes=SMALL_VMEM),
        name="mix",
    )(first_target, aperture_first, keep, got)
    swap = both([(t, t ^ 1) for t in range(NBLK)])
    mate = shift(mine, swap)
    moved = shift(
        jnp.concatenate([onward, mate[:128]], 0),
        both([(t, t + 2) for t in range(0, NBLK - 2, 2)] + [(t, t - 2) for t in range(3, NBLK, 2)]),
    )
    pairs = []
    for chip in range(2, NBLK // 2):
        at_bottom = chip % TOP_CHIPS < 2
        pairs.append((2 * chip + at_bottom, 2 * chip - 4))
    odd = lax.axis_index("track") % 2 == 1
    across = shift(jnp.where(odd, mate[:EXT], mine[:EXT]), both(pairs))
    swapped = shift(jnp.concatenate([moved[:192], across], 0), swap)
    return pl.pallas_call(
        look_kernel,
        out_shape=jax.ShapeDtypeStruct((4, 128), F32),
        in_specs=[vm] * 6,
        out_specs=vm,
        compiler_params=pltpu.CompilerParams(vmem_limit_bytes=SMALL_VMEM),
        name="look",
    )(look_start.reshape(1, 4), own, mine, mate, moved, swapped)


def solution(mesh):
    consts = [jnp.asarray(t) for t in tables()]
    body = functools.partial(per_device, *consts)
    return jax.shard_map(
        body,
        mesh=mesh,
        in_specs=(P(("track", "section"), None), P("track"), P("track"), P("track")),
        out_specs=P("track", "section"),
        check_vma=False,
    )
```

```python
import functools
import math

import jax
import jax.numpy as jnp
import numpy as np
from jax import lax
from jax.experimental import pallas as pl
from jax.experimental.pallas import tpu as pltpu
from jax.sharding import PartitionSpec as P

SAMP = 256
ECH_DEV = 384
TB = 32
LOOK = 16
NBLK = 64
STEP = ECH_DEV // TB
HALF = ECH_DEV // 2
SUB = HALF // STEP
ROWS = 192
WINDOWS = 2
WROWS = ROWS // WINDOWS
NFFT = WROWS + SUB
CHUNK = 16
CHUNKS = WINDOWS * NFFT // CHUNK
WIN = 80
EXT = 48
VGRP = 4
TOP_CHIPS = 8
FWD_AT = 512
INV_AT = FWD_AT + VGRP * NFFT
RANGE_AT = INV_AT + 2 * WROWS
TAB_END = RANGE_AT + 512
FOCUS_VMEM = 54912 * 1024
SMALL_VMEM = 8 * 1024 * 1024
BF = jnp.bfloat16
F32 = jnp.float32


def split_bf16(x):
    hi = x.astype(np.float32).astype(jnp.bfloat16)
    lo = (x - hi.astype(np.float64)).astype(np.float32).astype(jnp.bfloat16)
    return np.stack([hi, lo])


@functools.lru_cache(maxsize=None)
def tables():
    s = np.arange(SAMP)
    psi = -math.pi * 0.37 * (s - SAMP // 2) ** 2 / SAMP
    turns = np.outer(s, s) % SAMP
    comp = np.exp(1j * psi)[:, None] * np.exp(-2j * math.pi * turns / SAMP) / math.sqrt(SAMP)
    comp = split_bf16(np.concatenate([comp.real, comp.imag], 1))

    w = np.arange(NFFT)
    u = np.arange(SUB)
    fwd = np.exp(-2j * math.pi * (np.outer(w, u) % NFFT) / NFFT)
    cols = [[fwd.real, -fwd.imag], [fwd.imag, fwd.real]]
    lhs = np.zeros((VGRP, 2, NFFT, 2, VGRP, SUB))
    for v in range(VGRP):
        for o in range(2):
            for c in range(2):
                lhs[v, o, :, c, v, :] = cols[o][c]
    lhs = lhs.reshape(VGRP * 2 * NFFT, 2 * VGRP * SUB)
    hl = split_bf16(lhs)
    fwd_table = np.concatenate([hl[0], hl[1]], 1)

    f = np.arange(SAMP)
    kappa = 568.6 + (f - SAMP // 2) * 13.4 / SAMP
    resp = []
    for sec in range(2):
        for win in range(WINDOWS):
            m = np.arange(-WROWS, SUB)
            j = sec * SUB + 64 - win * WROWS + m
            dist = (STEP * j[None, :] + np.arange(STEP)[:, None]) * (1200.0 / ECH_DEV)
            delay = dist * dist / (np.sqrt(1.3e6 * 1.3e6 + dist * dist) + 1.3e6)
            h = np.exp(-1j * delay[:, :, None] * kappa)
            h = np.roll(h, -WROWS, axis=1)
            spec = np.fft.ifft(h, axis=1) / math.sqrt(4 * ECH_DEV)
            parts = np.stack([spec.real, spec.imag], 1)
            parts = parts.reshape(STEP, 2, NFFT // CHUNK, CHUNK, SAMP)
            resp.append(parts.transpose(2, 0, 1, 3, 4).reshape(NFFT // CHUNK, STEP * 2 * CHUNK, SAMP))
    resp = np.stack(resp).astype(np.float32).reshape(2, CHUNKS, STEP * 2 * CHUNK, SAMP)

    r = np.arange(WROWS)
    inv = np.exp(2j * math.pi * (np.outer(r, w) % NFFT) / NFFT)
    inv = np.block([[inv.real, -inv.imag], [inv.imag, inv.real]])
    inv_table = np.zeros((2 * WROWS, 2, SAMP), jnp.bfloat16)
    inv_table[:, :, : 2 * NFFT] = split_bf16(inv).transpose(1, 0, 2)

    base = np.exp(2j * math.pi * turns / SAMP) / math.sqrt(SAMP)
    range_table = split_bf16(np.concatenate([base.real, base.imag], 1))
    fwd_table = np.concatenate([fwd_table[: VGRP * NFFT], fwd_table[VGRP * NFFT :]], 1)
    packed = [comp, fwd_table, inv_table, range_table]
    return np.concatenate([t.reshape(-1, 512) for t in packed], 0), resp


def dot(a, b):
    return jnp.dot(a, b, preferred_element_type=F32)


def complex_dot(parts, table):
    rows = table.shape[0] // 2
    re, im = parts
    sums = []
    for part in (re, im):
        total = dot(part[0], table[:rows]) + dot(part[0], table[rows:])
        if len(part) > 1:
            total = total + dot(part[1], table[:rows])
        sums.append(total)
    width = table.shape[1] // 2
    return sums[0][:, :width] - sums[1][:, width:], sums[0][:, width:] + sums[1][:, :width]


def hi_lo(x):
    hi = x.astype(BF)
    return hi, (x - hi.astype(F32)).astype(BF)


def focus_kernel(
    raw_hbm, tab_hbm, resp_hbm,
    send, keep,
    raw, comp_t, fwd_t, resp, inv_t, range_t, comp, rhs, spec, img, sems,
):
    section = lax.axis_index("section")
    chunks = CHUNKS
    pairs = [(raw_hbm, raw), (tab_hbm.at[:FWD_AT], comp_t), (tab_hbm.at[FWD_AT:INV_AT], fwd_t)]
    pairs += [(resp_hbm.at[section, i], resp.at[i]) for i in range(chunks)]
    pairs += [(tab_hbm.at[INV_AT:RANGE_AT], inv_t), (tab_hbm.at[RANGE_AT:TAB_END], range_t)]
    pairs = pairs[:3] + pairs[-2:] + pairs[3:-2]
    copies = [pltpu.make_async_copy(src, dst, sems.at[i]) for i, (src, dst) in enumerate(pairs)]
    for copy in copies:
        copy.start()
    copies[0].wait()
    copies[1].wait()
    echo_re, echo_im = complex_dot([(raw[:, :SAMP],), (raw[:, SAMP:],)], comp_t[...])
    for n in range(2):
        comp[n, :HALF] = echo_re[:, n * 128 : n * 128 + 128]
        comp[2 + n, :HALF] = echo_im[:, n * 128 : n * 128 + 128]
    for v in range(STEP):
        rows = [comp[n, pl.ds(v, SUB, stride=STEP), :].astype(BF) for n in range(4)]
        q, i = divmod(v, VGRP)
        for c in range(2):
            part = jnp.concatenate(rows[2 * c : 2 * c + 2], 1)
            for d in range(2):
                at = ((d * 2 + c) * VGRP + i) * SUB
                rhs[q, at : at + SUB, :] = part
    copies[2].wait()
    for q in range(STEP // VGRP):
        for n in range(2):
            spec[q, n * VGRP * NFFT : (n + 1) * VGRP * NFFT] = dot(fwd_t[:, n * SAMP : (n + 1) * SAMP], rhs[q])
    copies[3].wait()
    copies[4].wait()
    inv_hi = inv_t[:, : 2 * NFFT]
    inv_lo = inv_t[:, SAMP : SAMP + 2 * NFFT]
    image = []
    for i in range(chunks):
        win, j = divmod(i, NFFT // CHUNK)
        copies[5 + i].wait()
        sum_re = jnp.zeros((CHUNK, SAMP), F32)
        sum_im = jnp.zeros((CHUNK, SAMP), F32)
        for v in range(STEP):
            q, k = divmod(v, VGRP)
            at = k * 2 * NFFT + j * CHUNK
            y_re = spec[q, at : at + CHUNK, :]
            y_im = spec[q, at + NFFT : at + NFFT + CHUNK, :]
            h_re = resp[i, v * 2 * CHUNK : v * 2 * CHUNK + CHUNK, :]
            h_im = resp[i, v * 2 * CHUNK + CHUNK : (v + 1) * 2 * CHUNK, :]
            sum_re += y_re * h_re - y_im * h_im
            sum_im += y_re * h_im + y_im * h_re
        for n, total in enumerate((sum_re, sum_im)):
            at = n * NFFT + j * CHUNK
            img[win, 0, at : at + CHUNK, :], img[win, 1, at : at + CHUNK, :] = hi_lo(total)
        if j == NFFT // CHUNK - 1:
            image.append(dot(inv_hi, img[win, 0]) + (dot(inv_lo, img[win, 0]) + dot(inv_hi, img[win, 1])))
    image_re = jnp.concatenate([part[:WROWS] for part in image], 0)
    image_im = jnp.concatenate([part[WROWS:] for part in image], 0)
    field_re, field_im = complex_dot([hi_lo(image_re), hi_lo(image_im)], range_t[...])
    low = jnp.concatenate([field_re[:, :128], field_im[:, :128]], 1)
    high = jnp.concatenate([field_re[:, 128:], field_im[:, 128:]], 1)

    @pl.when(section == 0)
    def low_half():
        send[...] = high.astype(BF)
        keep[...] = low

    @pl.when(section == 1)
    def high_half():
        send[...] = low.astype(BF)
        keep[...] = high


def mix_kernel(first_ref, low_ref, keep, got, own, mine, onward):
    block = lax.axis_index("track")
    lane = lax.broadcasted_iota(jnp.int32, (16, SAMP), 1)
    info = jnp.where(lane < 128, first_ref[0] - block * TB, low_ref[0] - block + 2)
    field = keep[...] + got[...].astype(F32)
    own[...] = field[64 : 64 + WIN]
    mine[112:128, :] = info.astype(F32).astype(BF)

    @pl.when(block % 2 == 0)
    def even():
        onward[...] = field[112:].astype(BF)
        mine[:112, :] = field[:112].astype(BF)
        mine[128:, :] = field[96:176].astype(BF)

    @pl.when(block % 2 == 1)
    def odd():
        onward[...] = field[:80].astype(BF)
        mine[:112, :] = field[80:].astype(BF)
        mine[128:, :] = field[32:112].astype(BF)


def look_kernel(starts, own, mine, mate, moved, swapped, looks):
    block = lax.axis_index("track")
    even = block % 2 == 0
    near = mate[128:, :].astype(F32)
    below = jnp.where(even, moved[96:176, :].astype(F32), near)
    above = jnp.where(even, near, moved[112:192, :].astype(F32))
    two_down = jnp.where(even, moved[16:80, :].astype(F32), swapped[128:192, :].astype(F32))
    two_up = jnp.where(even, swapped[80:160, :].astype(F32), moved[:80, :].astype(F32))
    far = jnp.where(even, swapped[:EXT, :].astype(F32), swapped[192:, :].astype(F32))
    next_info = jnp.where(even, mate[112:128, :].astype(F32), moved[192:, :].astype(F32))
    own_info = mine[112:128, :].astype(F32)
    first, next_first = own_info[0:1, :128], next_info[0:1, :128]
    low, next_low = own_info[0:1, 128:] < 0.5, next_info[0:1, 128:] < 0.5
    low = jnp.concatenate([low, low], 1)
    next_low = jnp.concatenate([next_low, next_low], 1)
    here = own[...]
    window = below[:64] + here[:64] + above[:64] + jnp.where(low, two_down, two_up[:64])
    beyond = here[32:] + above[32:] + two_up[32:] + jnp.where(next_low, below[32:], far)
    field = jnp.concatenate([window, beyond], 0)
    power = field[:, :128] * field[:, :128] + field[:, 128:] * field[:, 128:]
    row = lax.broadcasted_iota(jnp.int32, (64 + EXT, 128), 0)
    inner = row - first.astype(jnp.int32)
    outer = row - 64 - next_first.astype(jnp.int32) + TB
    inner = jnp.where((inner >= 0) & (inner < TB), inner, -1)
    outer = jnp.where((outer >= TB) & (block < NBLK - 1), outer, -1)
    place = jnp.where(row < 64, inner, outer)
    out = []
    for k in range(4):
        start = starts[:, k : k + 1] - block * TB
        inside = (place >= start) & (place < start + LOOK)
        out.append(jnp.sum(jnp.where(inside, power, 0.0), 0, keepdims=True))
    looks[...] = jnp.concatenate(out, 0) * (1.0 / LOOK)


def shift(value, pairs):
    return lax.ppermute(value, ("section", "track"), pairs)


def both(pairs):
    return [(s * NBLK + a, s * NBLK + b) for s in range(2) for a, b in pairs]


def per_device(tab, resp, raw, first_target, aperture_first, look_start):
    vm = pl.BlockSpec(memory_space=pltpu.VMEM)
    sm = pl.BlockSpec(memory_space=pltpu.SMEM)
    hbm = pl.BlockSpec(memory_space=pltpu.HBM)
    send, keep = pl.pallas_call(
        focus_kernel,
        out_shape=[
            jax.ShapeDtypeStruct((ROWS, SAMP), BF),
            jax.ShapeDtypeStruct((ROWS, SAMP), F32),
        ],
        in_specs=[hbm] * 3,
        out_specs=[vm] * 2,
        scratch_shapes=[
            pltpu.VMEM((HALF, 512), BF),
            pltpu.VMEM((FWD_AT, 512), BF),
            pltpu.VMEM((VGRP * NFFT, 512), BF),
            pltpu.VMEM((CHUNKS, STEP * 2 * CHUNK, SAMP), F32),
            pltpu.VMEM((2 * WROWS, 512), BF),
            pltpu.VMEM((512, 512), BF),
            pltpu.VMEM((4, HALF + 2 * CHUNK, 128), F32),
            pltpu.VMEM((STEP // VGRP, 256, SAMP), BF),
            pltpu.VMEM((STEP // VGRP, VGRP * 2 * NFFT, SAMP), F32),
            pltpu.VMEM((WINDOWS, 2, 2 * NFFT, SAMP), BF),
            pltpu.SemaphoreType.DMA((CHUNKS + 5,)),
        ],
        compiler_params=pltpu.CompilerParams(vmem_limit_bytes=FOCUS_VMEM),
        name="focus",
    )(raw, tab, resp)
    first_target, aperture_first, look_start, keep = lax.optimization_barrier(
        (first_target, aperture_first, look_start, keep)
    )
    got = shift(send, [(s * NBLK + t, (1 - s) * NBLK + t) for s in range(2) for t in range(NBLK)])
    own, mine, onward = pl.pallas_call(
        mix_kernel,
        out_shape=[
            jax.ShapeDtypeStruct((WIN, SAMP), F32),
            jax.ShapeDtypeStruct((208, SAMP), BF),
            jax.ShapeDtypeStruct((80, SAMP), BF),
        ],
        in_specs=[sm] * 2 + [vm] * 2,
        out_specs=[vm] * 3,
        compiler_params=pltpu.CompilerParams(vmem_limit_bytes=SMALL_VMEM),
        name="mix",
    )(first_target, aperture_first, keep, got)
    swap = both([(t, t ^ 1) for t in range(NBLK)])
    mate = shift(mine, swap)
    moved = shift(
        jnp.concatenate([onward, mate[:128]], 0),
        both([(t, t + 2) for t in range(0, NBLK - 2, 2)] + [(t, t - 2) for t in range(3, NBLK, 2)]),
    )
    pairs = []
    for chip in range(2, NBLK // 2):
        at_bottom = chip % TOP_CHIPS < 2
        pairs.append((2 * chip + at_bottom, 2 * chip - 4))
    odd = lax.axis_index("track") % 2 == 1
    across = shift(jnp.where(odd, mate[:EXT], mine[:EXT]), both(pairs))
    swapped = shift(jnp.concatenate([moved[:192], across], 0), swap)
    return pl.pallas_call(
        look_kernel,
        out_shape=jax.ShapeDtypeStruct((4, 128), F32),
        in_specs=[vm] * 6,
        out_specs=vm,
        compiler_params=pltpu.CompilerParams(vmem_limit_bytes=SMALL_VMEM),
        name="look",
    )(look_start.reshape(1, 4), own, mine, mate, moved, swapped)


def solution(mesh):
    consts = [jnp.asarray(t) for t in tables()]
    body = functools.partial(per_device, *consts)
    return jax.shard_map(
        body,
        mesh=mesh,
        in_specs=(P(("track", "section"), None), P("track"), P("track"), P("track")),
        out_specs=P("track", "section"),
        check_vma=False,
    )
```

```python
import functools
import math

import jax
import jax.numpy as jnp
import numpy as np
from jax import lax
from jax.experimental import pallas as pl
from jax.experimental.pallas import tpu as pltpu
from jax.sharding import PartitionSpec as P

SAMP = 256
ECH_DEV = 384
TB = 32
LOOK = 16
NBLK = 64
STEP = ECH_DEV // TB
HALF = ECH_DEV // 2
SUB = HALF // STEP
ROWS = 192
WINDOWS = 2
WROWS = ROWS // WINDOWS
NFFT = WROWS + SUB
CHUNK = 16
CHUNKS = WINDOWS * NFFT // CHUNK
WIN = 80
EXT = 48
VGRP = 4
TOP_CHIPS = 8
FWD_AT = 512
INV_AT = FWD_AT + VGRP * NFFT
RANGE_AT = INV_AT + 2 * WROWS
TAB_END = RANGE_AT + 512
FOCUS_VMEM = 54912 * 1024
SMALL_VMEM = 8 * 1024 * 1024
BF = jnp.bfloat16
F32 = jnp.float32


def split_bf16(x):
    hi = x.astype(np.float32).astype(jnp.bfloat16)
    lo = (x - hi.astype(np.float64)).astype(np.float32).astype(jnp.bfloat16)
    return np.stack([hi, lo])


@functools.lru_cache(maxsize=None)
def tables():
    s = np.arange(SAMP)
    psi = -math.pi * 0.37 * (s - SAMP // 2) ** 2 / SAMP
    turns = np.outer(s, s) % SAMP
    comp = np.exp(1j * psi)[:, None] * np.exp(-2j * math.pi * turns / SAMP) / math.sqrt(SAMP)
    comp = split_bf16(np.concatenate([comp.real, comp.imag], 1))

    w = np.arange(NFFT)
    u = np.arange(SUB)
    fwd = np.exp(-2j * math.pi * (np.outer(w, u) % NFFT) / NFFT)
    cols = [[fwd.real, -fwd.imag], [fwd.imag, fwd.real]]
    lhs = np.zeros((VGRP, 2, NFFT, 2, VGRP, SUB))
    for v in range(VGRP):
        for o in range(2):
            for c in range(2):
                lhs[v, o, :, c, v, :] = cols[o][c]
    lhs = lhs.reshape(VGRP * 2 * NFFT, 2 * VGRP * SUB)
    hl = split_bf16(lhs)
    fwd_table = np.concatenate([hl[0], hl[1]], 1)

    f = np.arange(SAMP)
    kappa = 568.6 + (f - SAMP // 2) * 13.4 / SAMP
    resp = []
    for sec in range(2):
        for win in range(WINDOWS):
            m = np.arange(-WROWS, SUB)
            j = sec * SUB + 64 - win * WROWS + m
            dist = (STEP * j[None, :] + np.arange(STEP)[:, None]) * (1200.0 / ECH_DEV)
            delay = dist * dist / (np.sqrt(1.3e6 * 1.3e6 + dist * dist) + 1.3e6)
            h = np.exp(-1j * delay[:, :, None] * kappa)
            h = np.roll(h, -WROWS, axis=1)
            spec = np.fft.ifft(h, axis=1) / math.sqrt(4 * ECH_DEV)
            parts = np.stack([spec.real, spec.imag], 1)
            parts = parts.reshape(STEP, 2, NFFT // CHUNK, CHUNK, SAMP)
            resp.append(parts.transpose(2, 0, 1, 3, 4).reshape(NFFT // CHUNK, STEP * 2 * CHUNK, SAMP))
    resp = np.stack(resp).astype(np.float32).reshape(2, CHUNKS, STEP * 2 * CHUNK, SAMP)

    r = np.arange(WROWS)
    inv = np.exp(2j * math.pi * (np.outer(r, w) % NFFT) / NFFT)
    inv = np.block([[inv.real, -inv.imag], [inv.imag, inv.real]])
    inv_table = np.zeros((2 * WROWS, 2, SAMP), jnp.bfloat16)
    inv_table[:, :, : 2 * NFFT] = split_bf16(inv).transpose(1, 0, 2)

    base = np.exp(2j * math.pi * turns / SAMP) / math.sqrt(SAMP)
    range_table = split_bf16(np.concatenate([base.real, base.imag], 1))
    fwd_table = np.concatenate([fwd_table[: VGRP * NFFT], fwd_table[VGRP * NFFT :]], 1)
    packed = [comp, fwd_table, inv_table, range_table]
    return np.concatenate([t.reshape(-1, 512) for t in packed], 0), resp


def dot(a, b):
    return jnp.dot(a, b, preferred_element_type=F32)


def complex_dot(parts, table):
    rows = table.shape[0] // 2
    re, im = parts
    sums = []
    for part in (re, im):
        if len(part) > 1:
            total = dot(jnp.concatenate([part[0], *part], 1), jnp.concatenate([table, table[:rows]], 0))
        else:
            total = dot(jnp.concatenate([part[0], part[0]], 1), table)
        sums.append(total)
    width = table.shape[1] // 2
    return sums[0][:, :width] - sums[1][:, width:], sums[0][:, width:] + sums[1][:, :width]


def hi_lo(x):
    hi = x.astype(BF)
    return hi, (x - hi.astype(F32)).astype(BF)


def focus_kernel(
    raw_hbm, tab_hbm, resp_hbm,
    send, keep,
    raw, comp_t, fwd_t, resp, inv_t, range_t, comp, rhs, spec, img, sems,
):
    section = lax.axis_index("section")
    chunks = CHUNKS
    pairs = [(raw_hbm, raw), (tab_hbm.at[:FWD_AT], comp_t), (tab_hbm.at[FWD_AT:INV_AT], fwd_t)]
    pairs += [(resp_hbm.at[section, i], resp.at[i]) for i in range(chunks)]
    pairs += [(tab_hbm.at[INV_AT:RANGE_AT], inv_t), (tab_hbm.at[RANGE_AT:TAB_END], range_t)]
    pairs = pairs[:3] + pairs[-2:] + pairs[3:-2]
    copies = [pltpu.make_async_copy(src, dst, sems.at[i]) for i, (src, dst) in enumerate(pairs)]
    for copy in copies:
        copy.start()
    copies[0].wait()
    copies[1].wait()
    echo_re, echo_im = complex_dot([(raw[:, :SAMP],), (raw[:, SAMP:],)], comp_t[...])
    for n in range(2):
        comp[n, :HALF] = echo_re[:, n * 128 : n * 128 + 128]
        comp[2 + n, :HALF] = echo_im[:, n * 128 : n * 128 + 128]
    for v in range(STEP):
        rows = [comp[n, pl.ds(v, SUB, stride=STEP), :].astype(BF) for n in range(4)]
        q, i = divmod(v, VGRP)
        for c in range(2):
            part = jnp.concatenate(rows[2 * c : 2 * c + 2], 1)
            for d in range(2):
                at = ((d * 2 + c) * VGRP + i) * SUB
                rhs[q, at : at + SUB, :] = part
    copies[2].wait()
    for q in range(STEP // VGRP):
        for n in range(2):
            spec[q, n * VGRP * NFFT : (n + 1) * VGRP * NFFT] = dot(fwd_t[:, n * SAMP : (n + 1) * SAMP], rhs[q])
    copies[3].wait()
    copies[4].wait()
    inv_hi = inv_t[:, : 2 * NFFT]
    inv_lo = inv_t[:, SAMP : SAMP + 2 * NFFT]
    image = []
    for i in range(chunks):
        win, j = divmod(i, NFFT // CHUNK)
        copies[5 + i].wait()
        sum_re = jnp.zeros((CHUNK, SAMP), F32)
        sum_im = jnp.zeros((CHUNK, SAMP), F32)
        for v in range(STEP):
            q, k = divmod(v, VGRP)
            at = k * 2 * NFFT + j * CHUNK
            y_re = spec[q, at : at + CHUNK, :]
            y_im = spec[q, at + NFFT : at + NFFT + CHUNK, :]
            h_re = resp[i, v * 2 * CHUNK : v * 2 * CHUNK + CHUNK, :]
            h_im = resp[i, v * 2 * CHUNK + CHUNK : (v + 1) * 2 * CHUNK, :]
            sum_re += y_re * h_re - y_im * h_im
            sum_im += y_re * h_im + y_im * h_re
        for n, total in enumerate((sum_re, sum_im)):
            at = n * NFFT + j * CHUNK
            img[win, 0, at : at + CHUNK, :], img[win, 1, at : at + CHUNK, :] = hi_lo(total)
        if j == NFFT // CHUNK - 1:
            image.append(dot(inv_hi, img[win, 0]) + (dot(inv_lo, img[win, 0]) + dot(inv_hi, img[win, 1])))
    image_re = jnp.concatenate([part[:WROWS] for part in image], 0)
    image_im = jnp.concatenate([part[WROWS:] for part in image], 0)
    field_re, field_im = complex_dot([hi_lo(image_re), hi_lo(image_im)], range_t[...])
    low = jnp.concatenate([field_re[:, :128], field_im[:, :128]], 1)
    high = jnp.concatenate([field_re[:, 128:], field_im[:, 128:]], 1)

    @pl.when(section == 0)
    def low_half():
        send[...] = high.astype(BF)
        keep[...] = low

    @pl.when(section == 1)
    def high_half():
        send[...] = low.astype(BF)
        keep[...] = high


def mix_kernel(first_ref, low_ref, keep, got, own, mine, onward):
    block = lax.axis_index("track")
    lane = lax.broadcasted_iota(jnp.int32, (16, SAMP), 1)
    info = jnp.where(lane < 128, first_ref[0] - block * TB, low_ref[0] - block + 2)
    field = keep[...] + got[...].astype(F32)
    own[...] = field[64 : 64 + WIN]
    mine[112:128, :] = info.astype(F32).astype(BF)

    @pl.when(block % 2 == 0)
    def even():
        onward[...] = field[112:].astype(BF)
        mine[:112, :] = field[:112].astype(BF)
        mine[128:, :] = field[96:176].astype(BF)

    @pl.when(block % 2 == 1)
    def odd():
        onward[...] = field[:80].astype(BF)
        mine[:112, :] = field[80:].astype(BF)
        mine[128:, :] = field[32:112].astype(BF)


def look_kernel(starts, own, mine, mate, moved, swapped, looks):
    block = lax.axis_index("track")
    even = block % 2 == 0
    near = mate[128:, :].astype(F32)
    below = jnp.where(even, moved[96:176, :].astype(F32), near)
    above = jnp.where(even, near, moved[112:192, :].astype(F32))
    two_down = jnp.where(even, moved[16:80, :].astype(F32), swapped[128:192, :].astype(F32))
    two_up = jnp.where(even, swapped[80:160, :].astype(F32), moved[:80, :].astype(F32))
    far = jnp.where(even, swapped[:EXT, :].astype(F32), swapped[192:, :].astype(F32))
    next_info = jnp.where(even, mate[112:128, :].astype(F32), moved[192:, :].astype(F32))
    own_info = mine[112:128, :].astype(F32)
    first, next_first = own_info[0:1, :128], next_info[0:1, :128]
    low, next_low = own_info[0:1, 128:] < 0.5, next_info[0:1, 128:] < 0.5
    low = jnp.concatenate([low, low], 1)
    next_low = jnp.concatenate([next_low, next_low], 1)
    here = own[...]
    window = below[:64] + here[:64] + above[:64] + jnp.where(low, two_down, two_up[:64])
    beyond = here[32:] + above[32:] + two_up[32:] + jnp.where(next_low, below[32:], far)
    field = jnp.concatenate([window, beyond], 0)
    power = field[:, :128] * field[:, :128] + field[:, 128:] * field[:, 128:]
    row = lax.broadcasted_iota(jnp.int32, (64 + EXT, 128), 0)
    inner = row - first.astype(jnp.int32)
    outer = row - 64 - next_first.astype(jnp.int32) + TB
    inner = jnp.where((inner >= 0) & (inner < TB), inner, -1)
    outer = jnp.where((outer >= TB) & (block < NBLK - 1), outer, -1)
    place = jnp.where(row < 64, inner, outer)
    out = []
    for k in range(4):
        start = starts[:, k : k + 1] - block * TB
        inside = (place >= start) & (place < start + LOOK)
        out.append(jnp.sum(jnp.where(inside, power, 0.0), 0, keepdims=True))
    looks[...] = jnp.concatenate(out, 0) * (1.0 / LOOK)


def shift(value, pairs):
    return lax.ppermute(value, ("section", "track"), pairs)


def both(pairs):
    return [(s * NBLK + a, s * NBLK + b) for s in range(2) for a, b in pairs]


def per_device(tab, resp, raw, first_target, aperture_first, look_start):
    vm = pl.BlockSpec(memory_space=pltpu.VMEM)
    sm = pl.BlockSpec(memory_space=pltpu.SMEM)
    hbm = pl.BlockSpec(memory_space=pltpu.HBM)
    send, keep = pl.pallas_call(
        focus_kernel,
        out_shape=[
            jax.ShapeDtypeStruct((ROWS, SAMP), BF),
            jax.ShapeDtypeStruct((ROWS, SAMP), F32),
        ],
        in_specs=[hbm] * 3,
        out_specs=[vm] * 2,
        scratch_shapes=[
            pltpu.VMEM((HALF, 512), BF),
            pltpu.VMEM((FWD_AT, 512), BF),
            pltpu.VMEM((VGRP * NFFT, 512), BF),
            pltpu.VMEM((CHUNKS, STEP * 2 * CHUNK, SAMP), F32),
            pltpu.VMEM((2 * WROWS, 512), BF),
            pltpu.VMEM((512, 512), BF),
            pltpu.VMEM((4, HALF + 2 * CHUNK, 128), F32),
            pltpu.VMEM((STEP // VGRP, 256, SAMP), BF),
            pltpu.VMEM((STEP // VGRP, VGRP * 2 * NFFT, SAMP), F32),
            pltpu.VMEM((WINDOWS, 2, 2 * NFFT, SAMP), BF),
            pltpu.SemaphoreType.DMA((CHUNKS + 5,)),
        ],
        compiler_params=pltpu.CompilerParams(vmem_limit_bytes=FOCUS_VMEM),
        name="focus",
    )(raw, tab, resp)
    first_target, aperture_first, look_start, keep = lax.optimization_barrier(
        (first_target, aperture_first, look_start, keep)
    )
    got = shift(send, [(s * NBLK + t, (1 - s) * NBLK + t) for s in range(2) for t in range(NBLK)])
    own, mine, onward = pl.pallas_call(
        mix_kernel,
        out_shape=[
            jax.ShapeDtypeStruct((WIN, SAMP), F32),
            jax.ShapeDtypeStruct((208, SAMP), BF),
            jax.ShapeDtypeStruct((80, SAMP), BF),
        ],
        in_specs=[sm] * 2 + [vm] * 2,
        out_specs=[vm] * 3,
        compiler_params=pltpu.CompilerParams(vmem_limit_bytes=SMALL_VMEM),
        name="mix",
    )(first_target, aperture_first, keep, got)
    swap = both([(t, t ^ 1) for t in range(NBLK)])
    mate = shift(mine, swap)
    moved = shift(
        jnp.concatenate([onward, mate[:128]], 0),
        both([(t, t + 2) for t in range(0, NBLK - 2, 2)] + [(t, t - 2) for t in range(3, NBLK, 2)]),
    )
    pairs = []
    for chip in range(2, NBLK // 2):
        at_bottom = chip % TOP_CHIPS < 2
        pairs.append((2 * chip + at_bottom, 2 * chip - 4))
    odd = lax.axis_index("track") % 2 == 1
    across = shift(jnp.where(odd, mate[:EXT], mine[:EXT]), both(pairs))
    swapped = shift(jnp.concatenate([moved[:192], across], 0), swap)
    return pl.pallas_call(
        look_kernel,
        out_shape=jax.ShapeDtypeStruct((4, 128), F32),
        in_specs=[vm] * 6,
        out_specs=vm,
        compiler_params=pltpu.CompilerParams(vmem_limit_bytes=SMALL_VMEM),
        name="look",
    )(look_start.reshape(1, 4), own, mine, mate, moved, swapped)


def solution(mesh):
    consts = [jnp.asarray(t) for t in tables()]
    body = functools.partial(per_device, *consts)
    return jax.shard_map(
        body,
        mesh=mesh,
        in_specs=(P(("track", "section"), None), P("track"), P("track"), P("track")),
        out_specs=P("track", "section"),
        check_vma=False,
    )
```

```python
import functools
import math

import jax
import jax.numpy as jnp
import numpy as np
from jax import lax
from jax.experimental import pallas as pl
from jax.experimental.pallas import tpu as pltpu
from jax.sharding import PartitionSpec as P

SAMP = 256
ECH_DEV = 384
TB = 32
LOOK = 16
NBLK = 64
STEP = ECH_DEV // TB
HALF = ECH_DEV // 2
SUB = HALF // STEP
ROWS = 192
WINDOWS = 2
WROWS = ROWS // WINDOWS
NFFT = WROWS + SUB
CHUNK = 16
CHUNKS = WINDOWS * NFFT // CHUNK
WIN = 80
EXT = 48
VGRP = 4
TOP_CHIPS = 8
FWD_AT = 512
INV_AT = FWD_AT + VGRP * NFFT
RANGE_AT = INV_AT + 2 * WROWS
TAB_END = RANGE_AT + 512
FOCUS_VMEM = 54912 * 1024
SMALL_VMEM = 8 * 1024 * 1024
BF = jnp.bfloat16
F32 = jnp.float32


def split_bf16(x):
    hi = x.astype(np.float32).astype(jnp.bfloat16)
    lo = (x - hi.astype(np.float64)).astype(np.float32).astype(jnp.bfloat16)
    return np.stack([hi, lo])


@functools.lru_cache(maxsize=None)
def tables():
    s = np.arange(SAMP)
    psi = -math.pi * 0.37 * (s - SAMP // 2) ** 2 / SAMP
    turns = np.outer(s, s) % SAMP
    comp = np.exp(1j * psi)[:, None] * np.exp(-2j * math.pi * turns / SAMP) / math.sqrt(SAMP)
    comp = split_bf16(np.concatenate([comp.real, comp.imag], 1))

    w = np.arange(NFFT)
    u = np.arange(SUB)
    fwd = np.exp(-2j * math.pi * (np.outer(w, u) % NFFT) / NFFT)
    cols = [[fwd.real, -fwd.imag], [fwd.imag, fwd.real]]
    lhs = np.zeros((VGRP, 2, NFFT, 2, VGRP, SUB))
    for v in range(VGRP):
        for o in range(2):
            for c in range(2):
                lhs[v, o, :, c, v, :] = cols[o][c]
    lhs = lhs.reshape(VGRP * 2 * NFFT, 2 * VGRP * SUB)
    hl = split_bf16(lhs)
    fwd_table = np.concatenate([hl[0], hl[1]], 1)

    f = np.arange(SAMP)
    kappa = 568.6 + (f - SAMP // 2) * 13.4 / SAMP
    resp = []
    for sec in range(2):
        for win in range(WINDOWS):
            m = np.arange(-WROWS, SUB)
            j = sec * SUB + 64 - win * WROWS + m
            dist = (STEP * j[None, :] + np.arange(STEP)[:, None]) * (1200.0 / ECH_DEV)
            delay = dist * dist / (np.sqrt(1.3e6 * 1.3e6 + dist * dist) + 1.3e6)
            h = np.exp(-1j * delay[:, :, None] * kappa)
            h = np.roll(h, -WROWS, axis=1)
            spec = np.fft.ifft(h, axis=1) / math.sqrt(4 * ECH_DEV)
            parts = np.stack([spec.real, spec.imag], 1)
            parts = parts.reshape(STEP, 2, NFFT // CHUNK, CHUNK, SAMP)
            resp.append(parts.transpose(2, 0, 1, 3, 4).reshape(NFFT // CHUNK, STEP * 2 * CHUNK, SAMP))
    resp = np.stack(resp).astype(np.float32).reshape(2, CHUNKS, STEP * 2 * CHUNK, SAMP)

    r = np.arange(WROWS)
    inv = np.exp(2j * math.pi * (np.outer(r, w) % NFFT) / NFFT)
    inv = np.block([[inv.real, -inv.imag], [inv.imag, inv.real]])
    inv_table = np.zeros((2 * WROWS, 2, SAMP), jnp.bfloat16)
    inv_table[:, :, : 2 * NFFT] = split_bf16(inv).transpose(1, 0, 2)

    base = np.exp(2j * math.pi * turns / SAMP) / math.sqrt(SAMP)
    range_table = split_bf16(np.concatenate([base.real, base.imag], 1))
    fwd_table = np.concatenate([fwd_table[: VGRP * NFFT], fwd_table[VGRP * NFFT :]], 1)
    packed = [comp, fwd_table, inv_table, range_table]
    return np.concatenate([t.reshape(-1, 512) for t in packed], 0), resp


def dot(a, b):
    return jnp.dot(a, b, preferred_element_type=F32)


def complex_dot(parts, table):
    rows = table.shape[0] // 2
    re, im = parts
    sums = []
    for part in (re, im):
        if len(part) > 1:
            total = dot(jnp.concatenate([part[0], *part], 1), jnp.concatenate([table, table[:rows]], 0))
        else:
            total = dot(jnp.concatenate([part[0], part[0]], 1), table)
        sums.append(total)
    width = table.shape[1] // 2
    return sums[0][:, :width] - sums[1][:, width:], sums[0][:, width:] + sums[1][:, :width]


def hi_lo(x):
    hi = x.astype(BF)
    return hi, (x - hi.astype(F32)).astype(BF)


def focus_kernel(
    raw_hbm, tab_hbm, resp_hbm,
    send, keep,
    raw, comp_t, fwd_t, resp, inv_t, range_t, comp, rhs, spec, img, sems,
):
    section = lax.axis_index("section")
    chunks = CHUNKS
    pairs = [(raw_hbm, raw), (tab_hbm.at[:FWD_AT], comp_t), (tab_hbm.at[FWD_AT:INV_AT], fwd_t)]
    pairs += [(resp_hbm.at[section, i], resp.at[i]) for i in range(chunks)]
    pairs += [(tab_hbm.at[INV_AT:RANGE_AT], inv_t), (tab_hbm.at[RANGE_AT:TAB_END], range_t)]
    pairs = pairs[:3] + pairs[-2:] + pairs[3:-2]
    copies = [pltpu.make_async_copy(src, dst, sems.at[i]) for i, (src, dst) in enumerate(pairs)]
    for copy in copies:
        copy.start()
    copies[0].wait()
    copies[1].wait()
    echo_re, echo_im = complex_dot([(raw[:, :SAMP],), (raw[:, SAMP:],)], comp_t[...])
    for n in range(2):
        comp[n, :HALF] = echo_re[:, n * 128 : n * 128 + 128]
        comp[2 + n, :HALF] = echo_im[:, n * 128 : n * 128 + 128]
    for v in range(STEP):
        rows = [comp[n, pl.ds(v, SUB, stride=STEP), :].astype(BF) for n in range(4)]
        q, i = divmod(v, VGRP)
        for c in range(2):
            part = jnp.concatenate(rows[2 * c : 2 * c + 2], 1)
            for d in range(2):
                at = ((d * 2 + c) * VGRP + i) * SUB
                rhs[q, at : at + SUB, :] = part
    copies[2].wait()
    for q in range(STEP // VGRP):
        for n in range(2):
            spec[q, n * VGRP * NFFT : (n + 1) * VGRP * NFFT] = dot(fwd_t[:, n * SAMP : (n + 1) * SAMP], rhs[q])
    copies[3].wait()
    copies[4].wait()
    inv_hi = inv_t[:, : 2 * NFFT]
    inv_lo = inv_t[:, SAMP : SAMP + 2 * NFFT]
    image = []
    for i in range(chunks):
        win, j = divmod(i, NFFT // CHUNK)
        copies[5 + i].wait()
        sum_re = jnp.zeros((CHUNK, SAMP), F32)
        sum_im = jnp.zeros((CHUNK, SAMP), F32)
        for v in range(STEP):
            q, k = divmod(v, VGRP)
            at = k * 2 * NFFT + j * CHUNK
            y_re = spec[q, at : at + CHUNK, :]
            y_im = spec[q, at + NFFT : at + NFFT + CHUNK, :]
            h_re = resp[i, v * 2 * CHUNK : v * 2 * CHUNK + CHUNK, :]
            h_im = resp[i, v * 2 * CHUNK + CHUNK : (v + 1) * 2 * CHUNK, :]
            sum_re += y_re * h_re - y_im * h_im
            sum_im += y_re * h_im + y_im * h_re
        for n, total in enumerate((sum_re, sum_im)):
            at = n * NFFT + j * CHUNK
            img[win, 0, at : at + CHUNK, :], img[win, 1, at : at + CHUNK, :] = hi_lo(total)
        if j == NFFT // CHUNK - 1:
            image.append(dot(inv_hi, img[win, 0]) + (dot(inv_lo, img[win, 0]) + dot(inv_hi, img[win, 1])))
    image_re = jnp.concatenate([part[:WROWS] for part in image], 0)
    image_im = jnp.concatenate([part[WROWS:] for part in image], 0)
    field_re, field_im = complex_dot([hi_lo(image_re), hi_lo(image_im)], range_t[...])
    low = jnp.concatenate([field_re[:, :128], field_im[:, :128]], 1)
    high = jnp.concatenate([field_re[:, 128:], field_im[:, 128:]], 1)

    @pl.when(section == 0)
    def low_half():
        send[...] = high.astype(BF)
        keep[...] = low

    @pl.when(section == 1)
    def high_half():
        send[...] = low.astype(BF)
        keep[...] = high


def mix_kernel(first_ref, low_ref, keep, got, own, mine, onward):
    block = lax.axis_index("track")
    lane = lax.broadcasted_iota(jnp.int32, (16, SAMP), 1)
    info = jnp.where(lane < 128, first_ref[...] - block * TB, low_ref[...] - block + 2)
    field = keep[...] + got[...].astype(F32)
    own[...] = field[64 : 64 + WIN]
    mine[112:128, :] = info.astype(F32).astype(BF)

    @pl.when(block % 2 == 0)
    def even():
        onward[...] = field[112:].astype(BF)
        mine[:112, :] = field[:112].astype(BF)
        mine[128:, :] = field[96:176].astype(BF)

    @pl.when(block % 2 == 1)
    def odd():
        onward[...] = field[:80].astype(BF)
        mine[:112, :] = field[80:].astype(BF)
        mine[128:, :] = field[32:112].astype(BF)


def look_kernel(starts, own, mine, mate, moved, swapped, looks):
    block = lax.axis_index("track")
    even = block % 2 == 0
    near = mate[128:, :].astype(F32)
    below = jnp.where(even, moved[96:176, :].astype(F32), near)
    above = jnp.where(even, near, moved[112:192, :].astype(F32))
    two_down = jnp.where(even, moved[16:80, :].astype(F32), swapped[128:192, :].astype(F32))
    two_up = jnp.where(even, swapped[80:160, :].astype(F32), moved[:80, :].astype(F32))
    far = jnp.where(even, swapped[:EXT, :].astype(F32), swapped[192:, :].astype(F32))
    next_info = jnp.where(even, mate[112:128, :].astype(F32), moved[192:, :].astype(F32))
    own_info = mine[112:128, :].astype(F32)
    first, next_first = own_info[0:1, :128], next_info[0:1, :128]
    low, next_low = own_info[0:1, 128:] < 0.5, next_info[0:1, 128:] < 0.5
    low = jnp.concatenate([low, low], 1)
    next_low = jnp.concatenate([next_low, next_low], 1)
    here = own[...]
    window = below[:64] + here[:64] + above[:64] + jnp.where(low, two_down, two_up[:64])
    beyond = here[32:] + above[32:] + two_up[32:] + jnp.where(next_low, below[32:], far)
    field = jnp.concatenate([window, beyond], 0)
    power = field[:, :128] * field[:, :128] + field[:, 128:] * field[:, 128:]
    row = lax.broadcasted_iota(jnp.int32, (64 + EXT, 128), 0)
    inner = row - first.astype(jnp.int32)
    outer = row - 64 - next_first.astype(jnp.int32) + TB
    inner = jnp.where((inner >= 0) & (inner < TB), inner, -1)
    outer = jnp.where((outer >= TB) & (block < NBLK - 1), outer, -1)
    place = jnp.where(row < 64, inner, outer)
    out = []
    for k in range(4):
        start = starts[:, k : k + 1] - block * TB
        inside = (place >= start) & (place < start + LOOK)
        out.append(jnp.sum(jnp.where(inside, power, 0.0), 0, keepdims=True))
    looks[...] = jnp.concatenate(out, 0) * (1.0 / LOOK)


def shift(value, pairs):
    return lax.ppermute(value, ("section", "track"), pairs)


def both(pairs):
    return [(s * NBLK + a, s * NBLK + b) for s in range(2) for a, b in pairs]


def per_device(tab, resp, raw, first_target, aperture_first, look_start):
    vm = pl.BlockSpec(memory_space=pltpu.VMEM)
    sm = pl.BlockSpec(memory_space=pltpu.SMEM)
    hbm = pl.BlockSpec(memory_space=pltpu.HBM)
    send, keep = pl.pallas_call(
        focus_kernel,
        out_shape=[
            jax.ShapeDtypeStruct((ROWS, SAMP), BF),
            jax.ShapeDtypeStruct((ROWS, SAMP), F32),
        ],
        in_specs=[hbm] * 3,
        out_specs=[vm] * 2,
        scratch_shapes=[
            pltpu.VMEM((HALF, 512), BF),
            pltpu.VMEM((FWD_AT, 512), BF),
            pltpu.VMEM((VGRP * NFFT, 512), BF),
            pltpu.VMEM((CHUNKS, STEP * 2 * CHUNK, SAMP), F32),
            pltpu.VMEM((2 * WROWS, 512), BF),
            pltpu.VMEM((512, 512), BF),
            pltpu.VMEM((4, HALF + 2 * CHUNK, 128), F32),
            pltpu.VMEM((STEP // VGRP, 256, SAMP), BF),
            pltpu.VMEM((STEP // VGRP, VGRP * 2 * NFFT, SAMP), F32),
            pltpu.VMEM((WINDOWS, 2, 2 * NFFT, SAMP), BF),
            pltpu.SemaphoreType.DMA((CHUNKS + 5,)),
        ],
        compiler_params=pltpu.CompilerParams(vmem_limit_bytes=FOCUS_VMEM),
        name="focus",
    )(raw, tab, resp)
    first_target, aperture_first, look_start, keep = lax.optimization_barrier(
        (first_target, aperture_first, look_start, keep)
    )
    got = shift(send, [(s * NBLK + t, (1 - s) * NBLK + t) for s in range(2) for t in range(NBLK)])
    own, mine, onward = pl.pallas_call(
        mix_kernel,
        out_shape=[
            jax.ShapeDtypeStruct((WIN, SAMP), F32),
            jax.ShapeDtypeStruct((208, SAMP), BF),
            jax.ShapeDtypeStruct((80, SAMP), BF),
        ],
        in_specs=[vm] * 4,
        out_specs=[vm] * 3,
        compiler_params=pltpu.CompilerParams(vmem_limit_bytes=SMALL_VMEM),
        name="mix",
    )(first_target.reshape(1, 1), aperture_first.reshape(1, 1), keep, got)
    swap = both([(t, t ^ 1) for t in range(NBLK)])
    mate = shift(mine, swap)
    moved = shift(
        jnp.concatenate([onward, mate[:128]], 0),
        both([(t, t + 2) for t in range(0, NBLK - 2, 2)] + [(t, t - 2) for t in range(3, NBLK, 2)]),
    )
    pairs = []
    for chip in range(2, NBLK // 2):
        at_bottom = chip % TOP_CHIPS < 2
        pairs.append((2 * chip + at_bottom, 2 * chip - 4))
    odd = lax.axis_index("track") % 2 == 1
    across = shift(jnp.where(odd, mate[:EXT], mine[:EXT]), both(pairs))
    swapped = shift(jnp.concatenate([moved[:192], across], 0), swap)
    return pl.pallas_call(
        look_kernel,
        out_shape=jax.ShapeDtypeStruct((4, 128), F32),
        in_specs=[vm] * 6,
        out_specs=vm,
        compiler_params=pltpu.CompilerParams(vmem_limit_bytes=SMALL_VMEM),
        name="look",
    )(look_start.reshape(1, 4), own, mine, mate, moved, swapped)


def solution(mesh):
    consts = [jnp.asarray(t) for t in tables()]
    body = functools.partial(per_device, *consts)
    return jax.shard_map(
        body,
        mesh=mesh,
        in_specs=(P(("track", "section"), None), P("track"), P("track"), P("track")),
        out_specs=P("track", "section"),
        check_vma=False,
    )
```
